256 devices in a mesh: seq: 32 (over y, z), head: 8 (over x, core).
Axes of the slice: x: 4, y: 4, z: 8, core: 2. Of those that a mesh axis runs over, the one named last changes fastest.
Arguments:
- mixer_input: bfloat16 [8192, 8192], P('seq', 'head'), may hold values from -6 to 6
- gate_input: bfloat16 [8192, 8192], P('seq', 'head'), may hold values from -6 to 6
- input_b: bfloat16 [8192, 1024], P('seq', 'head'), may hold values from -6 to 6
- input_c: bfloat16 [8192, 1024], P('seq', 'head'), may hold values from -0.03125 to 0.03125
- log_decay: float32 [128, 8192], P('head', 'seq'), may hold values from -0.7 to 0
- skip_gain: float32 [128], P('head'), may hold values from 0.25 to 3.5
- norm_gain: float32 [8192], P('head'), may hold values from 0.25 to 1.75
- queries: bfloat16 [8192, 8192], P('seq', 'head'), may hold values from -20 to 20
- key_rows: bfloat16 [8192, 1024], P('seq', 'head'), may hold values from -20 to 20
- value_rows: bfloat16 [8192, 1024], P('seq', 'head'), may hold values from -6 to 6
Outputs:
- mixer_output: bfloat16 [8192, 8192], P('seq', 'head')
- attended: bfloat16 [8192, 8192], P('seq', 'head')
The draws below stay inside these ranges and needn't reach their ends.
All inputs are finite; a program needn't handle non-finite values.
Results may differ from the reference program's by a relative error of at most 0.022.
Values may be sent and summed in bfloat16 or wider, within the bound.
No kernel may reach another device: no remote copies, remote signals or barrier semaphores. Data moves between devices by JAX's collectives and lax.ppermute only.
A program may use at most 64 MiB of HBM per device.

```python
import math
import jax
import jax.numpy as jnp
from jax import lax

MIXER_HEADS = 128
HDIM = 64
STATE = 128
GROUPS = 8
QHEADS = 64
KVHEADS = 8
QDIM = 128
SPAN = 256
SEQUENCE_LENGTH = 8192


def drawn_rows(key):
    key_base = jax.random.fold_in(key, 0)
    base_keys = jax.random.truncated_normal(key_base, -4.0, 4.0, (SEQUENCE_LENGTH, KVHEADS, QDIM), jnp.float32)
    return base_keys


def draw_key_rows(key, part):
    base_keys = drawn_rows(key)
    sampled_values = base_keys
    return sampled_values.reshape(SEQUENCE_LENGTH, KVHEADS * QDIM).astype(jnp.bfloat16)


def draw_queries(key, part):
    key = jax.random.fold_in(key, 22)
    own_queries = jax.random.truncated_normal(key, -4.0, 4.0, (SEQUENCE_LENGTH, KVHEADS, QHEADS // KVHEADS, QDIM), jnp.float32)
    sampled_values = own_queries
    return sampled_values.reshape(SEQUENCE_LENGTH, QHEADS * QDIM).astype(jnp.bfloat16)


def draw_log_decay(key, part):
    key = jax.random.fold_in(key, 31)
    random_keys = jax.random.split(key, 9)
    fast_share = 0.5
    lower_edge = 0.5
    upper_edge = 2.0
    block_count = SEQUENCE_LENGTH // SPAN
    fast_heads = jax.random.uniform(random_keys[0], (MIXER_HEADS,)) < fast_share
    fast_rate = jnp.exp(jax.random.uniform(random_keys[1], (MIXER_HEADS,), minval=math.log(1.0 / 50.0), maxval=math.log(1.0 / 30.0)))
    slow_rate = jnp.exp(jax.random.uniform(random_keys[2], (MIXER_HEADS,), minval=math.log(0.05 / SEQUENCE_LENGTH), maxval=math.log(0.8 / SEQUENCE_LENGTH)))
    falloff_rate = jnp.where(fast_heads, fast_rate, slow_rate)
    jitter_level = jax.random.uniform(random_keys[3], (SEQUENCE_LENGTH, MIXER_HEADS), minval=lower_edge, maxval=upper_edge)
    busy_factor = jax.random.uniform(random_keys[4], (block_count, MIXER_HEADS), minval=0.5, maxval=1.5)
    quiet_factor = jnp.exp(jax.random.uniform(random_keys[7], (block_count, MIXER_HEADS), minval=math.log(0.02), maxval=math.log(0.1)))
    quiet_blocks = jax.random.uniform(random_keys[8], (block_count, MIXER_HEADS)) < 0.35
    spread_factor = jnp.where(quiet_blocks, quiet_factor, busy_factor)
    spread_factor = jnp.repeat(spread_factor, SPAN, axis=0)
    spike_rows = jax.random.uniform(random_keys[5], (SEQUENCE_LENGTH, 1)) < 3.0 / SEQUENCE_LENGTH
    spike_events = jax.random.uniform(random_keys[6], (SEQUENCE_LENGTH, MIXER_HEADS), minval=0.22, maxval=0.5)
    sampled_values = -(falloff_rate[None, :] * jitter_level * spread_factor + jnp.where(spike_rows, spike_events, 0.0))
    return sampled_values.T.astype(jnp.float32)


def draw_skip_gain(key, part):
    key = jax.random.fold_in(key, 41)
    rising = jnp.exp(jnp.linspace(math.log(0.5), math.log(2.0), MIXER_HEADS))
    jitter_level = jax.random.uniform(key, (MIXER_HEADS,), minval=0.8, maxval=1.25)
    return (rising * jitter_level).astype(jnp.float32)


def block_levels(stream_key, shape, pieces, low, top_value):
    factor_of = 1.0
    for axis_at, blocks in pieces:
        steps = jax.random.uniform(jax.random.fold_in(jax.random.fold_in(stream_key, 6), axis_at), (blocks,), jnp.float32, low / len(pieces), top_value / len(pieces))
        factor_of = factor_of * jnp.repeat(jnp.exp(steps), shape[axis_at] // blocks).reshape((-1,) + (1,) * (len(shape) - 1 - axis_at))
    return factor_of


def bell_draw(rng, shape, deviation, most, pieces=(), held_as=jnp.bfloat16):
    loudness = block_levels(rng, shape, pieces, -0.22, 0.18) if pieces else 1.0
    drawn = jax.random.normal(rng, shape, jnp.float32) * deviation * loudness
    return jnp.minimum(jnp.maximum(drawn, -most), most).astype(held_as)


def setup_inputs(seed: int = 0) -> dict:
    splits = jax.random.split(jax.random.key(seed), 11)
    return {
        "mixer_input": bell_draw(splits[0], (SEQUENCE_LENGTH, MIXER_HEADS * HDIM), 1.0, 6.0, ((0, 32), (1, 8))),
        "gate_input": bell_draw(splits[1], (SEQUENCE_LENGTH, MIXER_HEADS * HDIM), 1.0, 6.0, ((0, 32), (1, 8))),
        "input_b": bell_draw(splits[2], (SEQUENCE_LENGTH, GROUPS * STATE), 1.0, 6.0, ((0, 32), (1, 8))),
        "input_c": bell_draw(splits[3], (SEQUENCE_LENGTH, GROUPS * STATE), (STATE * SPAN) ** -0.5, 0.03125, ((0, 32), (1, 8))),
        "log_decay": draw_log_decay(jax.random.fold_in(splits[10], 71), 0),
        "skip_gain": draw_skip_gain(jax.random.fold_in(splits[10], 71), 0),
        "norm_gain": jnp.clip(1.0 + 0.15 * jax.random.normal(splits[6], (MIXER_HEADS * HDIM,), jnp.float32), 0.25, 1.75),
        "queries": draw_queries(jax.random.fold_in(splits[10], 71), 0),
        "key_rows": draw_key_rows(jax.random.fold_in(splits[10], 71), 0),
        "value_rows": bell_draw(splits[9], (SEQUENCE_LENGTH, KVHEADS * QDIM), 1.0, 6.0, ((0, 32), (1, 8))),
    }


EPSILON = 1e-05

def span_terms(block_x, block_b, block_c, block_decay, carry_state, skip_gain):
    head_count = block_decay.shape[1]
    group_count = block_b.shape[1]
    per_group = head_count // group_count
    cumulative = jnp.cumsum(block_decay, axis=0)
    block_total = cumulative[-1]
    wide_x = block_x.astype(jnp.float32)
    wide_b = block_b.astype(jnp.float32)
    wide_c = block_c.astype(jnp.float32)
    scores = jnp.einsum('tgn,sgn->gts', wide_c, wide_b)
    positions = jnp.arange(SPAN, dtype=jnp.int32)
    causal = positions[:, None] >= positions[None, :]
    across = cumulative.T
    spread_log = across[:, :, None] - across[:, None, :]
    decays = jnp.where(causal, jnp.exp(jnp.where(causal, spread_log, 0.0)), 0.0)
    weights = scores[:, None] * decays.reshape(group_count, per_group, SPAN, SPAN)
    weights = lax.optimization_barrier(weights.astype(jnp.bfloat16)).astype(jnp.float32)
    weights = weights.reshape(head_count, SPAN, SPAN)
    within = jnp.einsum('hts,shp->thp', weights, wide_x)
    scaled = wide_x * jnp.exp(block_total[None, :] - cumulative)[:, :, None]
    scaled = lax.optimization_barrier(scaled.astype(jnp.bfloat16)).astype(jnp.float32)
    block_state = jnp.einsum('sgip,sgn->gipn', scaled.reshape(SPAN, group_count, per_group, HDIM), wide_b)
    block_state = block_state.reshape(head_count, HDIM, STATE)
    carried = lax.optimization_barrier(carry_state.astype(jnp.bfloat16)).astype(jnp.float32)
    carried_term = jnp.einsum('tgn,gipn->tgip', wide_c, carried.reshape(group_count, per_group, HDIM, STATE))
    carried_term = carried_term.reshape(SPAN, head_count, HDIM) * jnp.exp(cumulative)[:, :, None]
    result = within + carried_term + skip_gain[None, :, None] * wide_x
    next_state = jnp.exp(block_total)[:, None, None] * carry_state + block_state
    return (next_state, result)

def attend_reference(queries, key_rows, value_rows):
    per_group = QHEADS // KVHEADS
    scale = QDIM ** (-0.5)
    query_heads = queries.reshape(SEQUENCE_LENGTH, QHEADS, QDIM)
    key_heads = key_rows.reshape(SEQUENCE_LENGTH, KVHEADS, QDIM)
    value_heads = value_rows.reshape(SEQUENCE_LENGTH, KVHEADS, QDIM)
    block_rows = min(512, SEQUENCE_LENGTH)
    key_positions = jnp.arange(SEQUENCE_LENGTH, dtype=jnp.int32)

    def one_head(head_number):
        query_block_all = lax.dynamic_index_in_dim(query_heads, head_number, 1, keepdims=False).astype(jnp.float32)
        group_number = (head_number // per_group).astype(jnp.int32)
        key_all = lax.dynamic_index_in_dim(key_heads, group_number, 1, keepdims=False).astype(jnp.float32)
        value_all = lax.dynamic_index_in_dim(value_heads, group_number, 1, keepdims=False).astype(jnp.float32)

        def one_block(first_row):
            query_block = lax.dynamic_slice_in_dim(query_block_all, first_row, block_rows, 0)
            query_positions = first_row + jnp.arange(block_rows, dtype=jnp.int32)
            allowed = key_positions[None, :] <= query_positions[:, None]
            logits = jnp.einsum('qd,kd->qk', query_block, key_all) * scale
            logits = jnp.where(allowed, logits, -1e+30)
            largest = lax.optimization_barrier(jnp.max(logits, axis=1, keepdims=True))
            probabilities = jnp.where(allowed, jnp.exp(logits - largest), 0.0)
            denominator = lax.optimization_barrier(jnp.sum(probabilities, axis=1, keepdims=True))
            rounded = lax.optimization_barrier(probabilities.astype(jnp.bfloat16)).astype(jnp.float32)
            return jnp.einsum('qk,kd->qd', rounded, value_all) / denominator
        starts = jnp.arange(0, SEQUENCE_LENGTH, block_rows, dtype=jnp.int32)
        return lax.map(one_block, starts).reshape(SEQUENCE_LENGTH, QDIM)
    per_head = lax.map(one_head, jnp.arange(QHEADS, dtype=jnp.int32))
    return jnp.transpose(per_head, (1, 0, 2)).reshape(SEQUENCE_LENGTH, QHEADS * QDIM).astype(jnp.bfloat16)

def reference(mixer_input, gate_input, input_b, input_c, log_decay, skip_gain, norm_gain, queries, key_rows, value_rows):
    block_count = SEQUENCE_LENGTH // SPAN
    x_blocks = mixer_input.reshape(block_count, SPAN, MIXER_HEADS, HDIM)
    b_blocks = input_b.reshape(block_count, SPAN, GROUPS, STATE)
    c_blocks = input_c.reshape(block_count, SPAN, GROUPS, STATE)
    decay_blocks = log_decay.T.reshape(block_count, SPAN, MIXER_HEADS)

    def advance(carry_state, block_item):
        block_x, block_b, block_c, block_decay = block_item
        return span_terms(block_x, block_b, block_c, block_decay, carry_state, skip_gain)
    initial = jnp.zeros((MIXER_HEADS, HDIM, STATE), jnp.float32)
    _, results = lax.scan(advance, initial, (x_blocks, b_blocks, c_blocks, decay_blocks))
    mixer_values = results.reshape(SEQUENCE_LENGTH, MIXER_HEADS * HDIM)
    gated = mixer_values * jax.nn.silu(gate_input.astype(jnp.float32))
    mean_square = lax.optimization_barrier(jnp.mean(gated * gated, axis=1, keepdims=True))
    mixer_output = (gated * lax.rsqrt(mean_square + EPSILON) * norm_gain[None, :]).astype(jnp.bfloat16)
    attended = attend_reference(queries, key_rows, value_rows)
    return (mixer_output, attended)
```

```python
import functools
import math

import jax
import jax.numpy as jnp
from jax import lax
from jax.experimental import pallas as pl
from jax.experimental.pallas import tpu as pltpu
from jax.sharding import PartitionSpec as P

STATE = 128
QDIM = 128
SPAN = 256
HALF = 128
EPSILON = 1e-05
SEQ_Y, SEQ_Z = 4, 8
LOGIT_SCALE = QDIM ** (-0.5) * math.log2(math.e)
HIGH = lax.Precision.HIGHEST
VMEM = pl.BlockSpec(memory_space=pltpu.VMEM)
SMEM = pl.BlockSpec(memory_space=pltpu.SMEM)
LIMIT = 40 * 2**20


def send(block, target):
    route = []
    for y in range(SEQ_Y):
        for z in range(SEQ_Z):
            to = target(y, z)
            if to is not None:
                route.append((y * SEQ_Z + z, to[0] * SEQ_Z + to[1]))
    return lax.ppermute(block, "seq", route)


def along_z(block, distance):
    return send(block, lambda y, z: (y, (z + distance) % SEQ_Z))


def along_y(block, distance):
    return send(block, lambda y, z: ((y + distance) % SEQ_Y, z))


def later_y(block, distance):
    return send(block, lambda y, z: (y + distance, z) if y + distance < SEQ_Y else None)


def across_z(block, bit):
    return send(block, lambda y, z: (y, z ^ bit))


def cost(flops, size, exps=0):
    return pl.CostEstimate(flops=flops, bytes_accessed=size, transcendentals=exps)


def prepare_kernel(key_ref, value_ref, first_ref, second_ref):
    first_ref[:, :QDIM] = key_ref[:HALF, :]
    first_ref[:, QDIM:] = value_ref[:HALF, :]
    second_ref[:, :QDIM] = key_ref[HALF:, :]
    second_ref[:, QDIM:] = value_ref[HALF:, :]


def prepare(key_rows, value_rows):
    half = jax.ShapeDtypeStruct((HALF, 2 * QDIM), jnp.bfloat16)
    return pl.pallas_call(
        prepare_kernel,
        out_shape=(half, half),
        in_specs=[VMEM, VMEM],
        out_specs=(VMEM, VMEM),
        cost_estimate=cost(0, 2**18),
        name="prepare",
    )(key_rows, value_rows)


def attend_kernel(segments, count, first, last, *refs):
    source_ref, query_ref = refs[0], refs[1]
    blocks = refs[2 : 2 + count]
    at = 2 + count
    if not first:
        at += 2
    max_ref, total_ref = refs[at : at + 2]
    wide_ref = refs[-1]
    heads = query_ref.shape[1] // QDIM
    rows = query_ref.shape[0]
    me = source_ref[0]
    my_y, my_z = lax.shift_right_logical(me, 3), lax.bitwise_and(me, SEQ_Z - 1)

    def source_of(place):
        up, along = place
        source_y = lax.bitwise_and(my_y + (up + SEQ_Y), SEQ_Y - 1)
        return source_y * SEQ_Z + lax.bitwise_and(my_z + (along + SEQ_Z), SEQ_Z - 1)

    if first:
        max_ref[...] = jnp.full(max_ref.shape, -1e30, jnp.float32)
        total_ref[...] = jnp.zeros(total_ref.shape, jnp.float32)
    wide_ref[:, QDIM:] = jnp.ones((wide_ref.shape[0], QDIM), jnp.bfloat16)

    def run(parts, masked):
        place = 0
        for which, offset, size, _, _ in parts:
            wide_ref[place : place + size, :QDIM] = blocks[which][offset : offset + size, QDIM:]
            place += size
        depth = place

        def one_head(head):
            columns = pl.ds(pl.multiple_of(head * QDIM, QDIM), QDIM)
            query = query_ref[:, columns]
            pieces = []
            for which, offset, size, source, shift in parts:
                keys = blocks[which][offset : offset + size, :QDIM]
                logits = lax.dot_general(
                    query, keys, (((1,), (1,)), ((), ())), preferred_element_type=jnp.float32
                )
                if masked:
                    kept = []
                    for n in range(size // HALF):
                        base = (source_of(source[n]) - me) * SPAN + shift
                        ahead = (
                            lax.broadcasted_iota(jnp.int32, (rows, HALF), 1)
                            - lax.broadcasted_iota(jnp.int32, (rows, HALF), 0)
                        )
                        part = logits[:, n * HALF : (n + 1) * HALF]
                        kept.append(jnp.where(ahead <= -base, part, -1e30))
                    pieces.extend(kept)
                else:
                    pieces.append(logits)
            logits = pieces[0] if len(pieces) == 1 else jnp.concatenate(pieces, axis=1)
            old = max_ref[head]
            new = jnp.maximum(old, jnp.max(logits, axis=1, keepdims=True))
            max_ref[head] = new
            scaled = new * LOGIT_SCALE
            rescale = jnp.exp2(old * LOGIT_SCALE - scaled)
            weights = jnp.exp2(logits * LOGIT_SCALE - scaled[:, :1]).astype(jnp.bfloat16)
            product = jnp.dot(
                weights, wide_ref[:depth, :], preferred_element_type=jnp.float32
            )
            total_ref[head] = total_ref[head] * rescale[:, :1] + product

        def two_heads(step, nothing):
            one_head(2 * step)
            one_head(2 * step + 1)
            return nothing

        lax.fori_loop(0, heads // 2, two_heads, 0)

    for parts in segments:
        whole = None
        some = None
        for _, _, size, source, _ in parts:
            for n in range(size // HALF):
                before = source_of(source[n]) < me
                upto = source_of(source[n]) <= me
                whole = before if whole is None else jnp.logical_and(whole, before)
                some = upto if some is None else jnp.logical_or(some, upto)
        pl.when(whole)(functools.partial(run, parts, False))
        pl.when(jnp.logical_and(some, jnp.logical_not(whole)))(functools.partial(run, parts, True))

    if last:
        out_ref = refs[at + 2]
        for head in range(heads):
            total = total_ref[head]
            out_ref[:, head * QDIM : (head + 1) * QDIM] = (
                total[:, :QDIM] / total[:, QDIM:]
            ).astype(jnp.bfloat16)


def attend_step(queries, here, segments, carry, last):
    blocks, described = [], []
    deepest = 0
    for segment in segments:
        parts = []
        for block, offset, size, from_blocks, shift in segment:
            at = next((n for n, b in enumerate(blocks) if b is block), None)
            if at is None:
                at = len(blocks)
                blocks.append(block)
            parts.append((at, offset, size, from_blocks, shift))
        described.append(parts)
        deepest = max(deepest, sum(part[2] for part in parts))
    first = carry is None
    rows, width = queries.shape
    heads = width // QDIM
    carry_shapes = (
        jax.ShapeDtypeStruct((heads, rows, QDIM), jnp.float32),
        jax.ShapeDtypeStruct((heads, rows, 2 * QDIM), jnp.float32),
    )
    keys = sum(part[2] for parts in described for part in parts)
    scratch = [pltpu.VMEM((deepest, 2 * QDIM), jnp.bfloat16)]
    operands = [here, queries, *blocks]
    aliases = {}
    if not first:
        aliases = {len(operands): 0, len(operands) + 1: 1}
        operands.extend(carry)
    out_shape = carry_shapes
    if last:
        out_shape = carry_shapes + (jax.ShapeDtypeStruct((rows, width), jnp.bfloat16),)
    outputs = pl.pallas_call(
        functools.partial(attend_kernel, described, len(blocks), first, last),
        out_shape=out_shape,
        in_specs=[SMEM] + [VMEM] * (len(operands) - 1),
        out_specs=(VMEM,) * len(out_shape),
        scratch_shapes=[pltpu.VMEM((deepest, 2 * QDIM), jnp.bfloat16)],
        input_output_aliases=aliases,
        compiler_params=pltpu.CompilerParams(vmem_limit_bytes=LIMIT),
        cost_estimate=cost(4 * rows * width * keys, 2 * rows * width, rows * heads * keys),
        name="attend",
    )(*operands)
    return outputs[2] if last else outputs


def spread(columns, pair):
    lanes = lax.broadcasted_iota(jnp.int32, (columns.shape[0], 128), 1)
    return jnp.where(lanes < 64, columns[:, 2 * pair : 2 * pair + 1], columns[:, 2 * pair + 1 : 2 * pair + 2])


def triangle(rows):
    down = lax.broadcasted_iota(jnp.int32, (rows, rows), 0)
    along = lax.broadcasted_iota(jnp.int32, (rows, rows), 1)
    return down >= along


def state_kernel(x_ref, b_ref, decay_ref, state_ref, fall_ref, columns_ref, scaled_ref):
    rows = x_ref.shape[0]
    lower = triangle(rows).astype(jnp.float32)
    columns = lax.dot_general(
        lower, decay_ref[...], (((1,), (1,)), ((), ())), precision=HIGH,
        preferred_element_type=jnp.float32,
    )
    columns_ref[...] = columns
    total = columns[rows - 1 : rows, :]
    remaining = jnp.exp(total - columns)
    fall = jnp.broadcast_to(jnp.exp(total), (8, total.shape[1]))
    for pair in range(x_ref.shape[1] // 128):
        at = slice(pair * 128, (pair + 1) * 128)
        scaled_ref[:, at] = (x_ref[:, at].astype(jnp.float32) * spread(remaining, pair)).astype(jnp.bfloat16)
        fall_ref[:, at] = spread(fall, pair)
    state_ref[...] = lax.dot_general(
        b_ref[...], scaled_ref[...], (((0,), (0,)), ((), ())), preferred_element_type=jnp.float32
    )


def block_states(x, b, decay):
    rows, width = x.shape
    heads = decay.shape[0]
    return pl.pallas_call(
        state_kernel,
        out_shape=(
            jax.ShapeDtypeStruct((STATE, width), jnp.float32),
            jax.ShapeDtypeStruct((8, width), jnp.float32),
            jax.ShapeDtypeStruct((rows, heads), jnp.float32),
        ),
        in_specs=[VMEM] * 3,
        out_specs=(VMEM,) * 3,
        scratch_shapes=[pltpu.VMEM((rows, width), jnp.bfloat16)],
        compiler_params=pltpu.CompilerParams(vmem_limit_bytes=LIMIT),
        cost_estimate=cost(2 * rows * width * STATE, 2**20),
        name="states",
    )(x, b, decay)


def within_kernel(x_ref, b_ref, c_ref, columns_ref, decay_ref, skip_ref, out_ref):
    rows = x_ref.shape[0]
    causal = triangle(rows)
    scores = lax.dot_general(
        c_ref[...], b_ref[...], (((1,), (1,)), ((), ())), preferred_element_type=jnp.float32
    )
    scores = jnp.where(causal, scores, 0.0)
    upper = jnp.where(causal, 0.0, 1.0) + jnp.where(
        lax.broadcasted_iota(jnp.int32, (rows, rows), 0) == lax.broadcasted_iota(jnp.int32, (rows, rows), 1), 1.0, 0.0
    )
    across = lax.dot_general(
        decay_ref[...], upper, (((1,), (0,)), ((), ())), precision=HIGH,
        preferred_element_type=jnp.float32,
    )
    columns = columns_ref[...]
    lanes = lax.broadcasted_iota(jnp.int32, (rows, 128), 1)
    for pair in range(x_ref.shape[1] // 128):
        at = slice(pair * 128, (pair + 1) * 128)
        x = x_ref[:, at]
        total = None
        for side in range(2):
            head = 2 * pair + side
            gap = jnp.minimum(columns[:, head : head + 1] - across[head : head + 1, :], 0.0)
            weights = (scores * jnp.exp(gap)).astype(jnp.bfloat16)
            mine = lanes < 64 if side == 0 else lanes >= 64
            product = jnp.dot(
                weights, jnp.where(mine, x, jnp.zeros_like(x)), preferred_element_type=jnp.float32
            )
            total = product if total is None else total + product
        out_ref[:, at] = total + skip_ref[:, at] * x.astype(jnp.float32)


def within_blocks(x, b, c, columns, decay, skip):
    rows, width = x.shape
    return pl.pallas_call(
        within_kernel,
        out_shape=jax.ShapeDtypeStruct((rows, width), jnp.float32),
        in_specs=[VMEM] * 6,
        out_specs=VMEM,
        compiler_params=pltpu.CompilerParams(vmem_limit_bytes=LIMIT),
        cost_estimate=cost(4 * rows * rows * width, 2**21, 2**20),
        name="within",
    )(x, b, c, columns, decay, skip)


def gate_kernel(within_ref, c_ref, carried_ref, columns_ref, gate_ref, gated_ref, squares_ref):
    grown = jnp.exp(columns_ref[...])
    total = None
    for pair in range(within_ref.shape[1] // 128):
        at = slice(pair * 128, (pair + 1) * 128)
        carried = jnp.dot(c_ref[...], carried_ref[:, at], preferred_element_type=jnp.float32)
        values = within_ref[:, at] + carried * spread(grown, pair)
        gate = gate_ref[:, at].astype(jnp.float32)
        gated = values * (gate / (1.0 + jnp.exp(-gate)))
        gated_ref[:, at] = gated
        total = gated * gated if total is None else total + gated * gated
    squares_ref[...] = lax.dot_general(
        jnp.ones((8, 128), jnp.float32), total, (((1,), (1,)), ((), ())), precision=HIGH,
        preferred_element_type=jnp.float32,
    )


def gate_values(within, c, carried, columns, gate):
    rows, width = within.shape
    return pl.pallas_call(
        gate_kernel,
        out_shape=(
            jax.ShapeDtypeStruct((rows, width), jnp.float32),
            jax.ShapeDtypeStruct((8, rows), jnp.float32),
        ),
        in_specs=[VMEM] * 5,
        out_specs=(VMEM, VMEM),
        compiler_params=pltpu.CompilerParams(vmem_limit_bytes=LIMIT),
        cost_estimate=cost(2 * rows * width * STATE, 2**21, 2**18),
        name="gating",
    )(within, c, carried, columns, gate)


def norm_kernel(full_width, gated_ref, squares_ref, gain_ref, out_ref):
    total = lax.dot_general(
        squares_ref[...], jnp.full((8, 128), 0.125, jnp.float32), (((0,), (0,)), ((), ())),
        precision=HIGH, preferred_element_type=jnp.float32,
    )
    factor = lax.rsqrt(total * (1.0 / full_width) + EPSILON)
    for pair in range(gated_ref.shape[1] // 128):
        at = slice(pair * 128, (pair + 1) * 128)
        out_ref[:, at] = (gated_ref[:, at] * factor * gain_ref[:, at]).astype(jnp.bfloat16)


def normalize(gated, squares, gain, full_width):
    rows, width = gated.shape
    return pl.pallas_call(
        functools.partial(norm_kernel, full_width),
        out_shape=jax.ShapeDtypeStruct((rows, width), jnp.bfloat16),
        in_specs=[VMEM] * 3,
        out_specs=VMEM,
        compiler_params=pltpu.CompilerParams(vmem_limit_bytes=LIMIT),
        cost_estimate=cost(4 * rows * width, 2**21),
        name="normalize",
    )(gated, squares, gain)


def packed(state, fall):
    high = lax.reduce_precision(fall, 8, 7)
    return jnp.concatenate([state, high, fall - high], axis=0).astype(jnp.bfloat16)


def unpacked(message):
    wide = message.astype(jnp.float32)
    return wide[:STATE], wide[STATE : STATE + 8] + wide[STATE + 8 : STATE + 16]


def entering_state(state, fall, me):
    kept = []
    for level in range(3):
        upper = (me >> level) & 1 == 1
        width = state.shape[1] // 2
        low, high = state[:, :width], state[:, width:]
        fall_low, fall_high = fall[:, :width], fall[:, width:]
        mine, mine_fall = jnp.where(upper, high, low), jnp.where(upper, fall_high, fall_low)
        message = packed(jnp.where(upper, low, high), jnp.where(upper, fall_low, fall_high))
        theirs, their_fall = unpacked(across_z(message, 1 << level))
        before, after = jnp.where(upper, theirs, mine), jnp.where(upper, mine, theirs)
        before_fall = jnp.where(upper, their_fall, mine_fall)
        after_fall = jnp.where(upper, mine_fall, their_fall)
        kept.append((upper, before, before_fall))
        state = after_fall[:1] * before + after
        fall = before_fall * after_fall
    message = packed(state, fall)
    one, one_fall = unpacked(later_y(message, 1))
    two, two_fall = unpacked(later_y(message, 2))
    three, _ = unpacked(later_y(message, 3))
    entering = one + one_fall[:1] * (two + two_fall[:1] * three)
    for level in reversed(range(3)):
        upper, before, before_fall = kept[level]
        second = before_fall[:1] * entering + before
        mine = jnp.where(upper, second, entering)
        other = jnp.where(upper, entering, second).astype(jnp.bfloat16)
        received = across_z(other, 1 << level).astype(jnp.float32)
        entering = jnp.where(
            upper,
            jnp.concatenate([received, mine], axis=1),
            jnp.concatenate([mine, received], axis=1),
        )
    return entering.astype(jnp.bfloat16)


def sum_over_heads(squares):
    devices = lax.axis_size("head")
    bit = 1
    while bit < devices:
        route = [(i, i ^ bit) for i in range(devices)]
        squares = squares + lax.ppermute(squares, "head", route)
        bit *= 2
    return squares


def body(
    mixer_input, gate_input, input_b, input_c, log_decay, skip_gain, norm_gain, queries, key_rows, value_rows
):
    me = lax.axis_index("seq").astype(jnp.int32)
    here = me[None]
    head_width = mixer_input.shape[1] // skip_gain.shape[0]
    full_width = mixer_input.shape[1] * lax.axis_size("head")

    first, second = prepare(key_rows, value_rows)
    state, fall, columns = block_states(mixer_input, input_b, log_decay)

    second_up, second_down = along_y(second, 1), along_y(second, -1)
    first_up, first_down = [first], [first]
    for step in range(4):
        first_up.append(along_z(first_up[-1], 1))
        if step < 3:
            first_down.append(along_z(first_down[-1], -1))
    second_two = along_y(second_up, 1)
    second_column = jnp.concatenate([second, second_up, second_two, second_down], axis=0)
    first_row = jnp.concatenate(first_up + first_down[1:], axis=0)
    row_z = [0, -1, -2, -3, -4, 1, 2, 3]

    def row_sources(up):
        return [(up, z) for z in row_z]

    def column_sources(z):
        return [(-up, z) for up in range(SEQ_Y)]

    row_up, row_down = along_y(first_row, 1), along_y(first_row, -1)
    middle = first_row.shape[0] // 2
    row_two = (along_y(row_up[:middle], 1), along_y(row_down[middle:], -1))
    column_up, column_down = [second_column], [second_column]
    for step in range(4):
        column_up.append(along_z(column_up[-1], 1))
        if step < 3:
            column_down.append(along_z(column_down[-1], -1))

    carry = attend_step(
        queries, here, [[(first, 0, HALF, [(0, 0)], 0), (second, 0, HALF, [(0, 0)], HALF)]], None, False
    )
    within = within_blocks(
        mixer_input, input_b, input_c, columns, log_decay, jnp.repeat(skip_gain, head_width)[None, :]
    )
    carried = entering_state(state, fall, me)

    own = column_sources(0)
    carry = attend_step(
        queries,
        here,
        [
            [(first_row, HALF, 7 * HALF, row_sources(0)[1:], 0)],
            [(second_column, HALF, 3 * HALF, own[1:], HALF)],
        ],
        carry,
        False,
    )

    def ring_segments(step):
        up = column_sources(-step)
        parts = [(column_up[step], up)]
        if step < 4:
            parts.append((column_down[step], column_sources(step)))
        return [
            [(block, HALF, 3 * HALF, where[1:], HALF) for block, where in parts],
            [(block, 0, HALF, where[:1], HALF) for block, where in parts],
        ]

    carry = attend_step(queries, here, ring_segments(1), carry, False)
    up_sources, down_sources = row_sources(-1), row_sources(1)
    carry = attend_step(
        queries, here, [[(row_up, 0, 8 * HALF, up_sources, 0)], [(row_down, 0, 8 * HALF, down_sources, 0)]], carry, False
    )
    carry = attend_step(queries, here, ring_segments(2), carry, False)
    two = row_sources(2)
    carry = attend_step(
        queries,
        here,
        [[(row_two[0], 0, middle, two[:4], 0), (row_two[1], 0, middle, two[4:], 0)]] + ring_segments(3),
        carry,
        False,
    )
    attended = attend_step(queries, here, ring_segments(4), carry, True)

    gated, squares = gate_values(within, input_c, carried, columns, gate_input)
    squares = sum_over_heads(squares)
    mixer_output = normalize(gated, squares, norm_gain[None, :], full_width)
    return (mixer_output, attended)


def solution(mesh):
    return jax.shard_map(
        body,
        mesh=mesh,
        in_specs=(
            P("seq", "head"),
            P("seq", "head"),
            P("seq", "head"),
            P("seq", "head"),
            P("head", "seq"),
            P("head"),
            P("head"),
            P("seq", "head"),
            P("seq", "head"),
            P("seq", "head"),
        ),
        out_specs=(P("seq", "head"), P("seq", "head")),
        check_vma=False,
    )
```

```python
import functools
import math

import jax
import jax.numpy as jnp
from jax import lax
from jax.experimental import pallas as pl
from jax.experimental.pallas import tpu as pltpu
from jax.sharding import PartitionSpec as P

STATE = 128
QDIM = 128
SPAN = 256
EPSILON = 1e-05
SEQ_Y, SEQ_Z = 4, 8
LOGIT_SCALE = QDIM ** (-0.5) * math.log2(math.e)
HIGH = lax.Precision.HIGHEST
VMEM = pl.BlockSpec(memory_space=pltpu.VMEM)
ANY = pl.BlockSpec(memory_space=pl.ANY)
SMEM = pl.BlockSpec(memory_space=pltpu.SMEM)
LIMIT = 40 * 2**20


def send(block, target):
    route = []
    for y in range(SEQ_Y):
        for z in range(SEQ_Z):
            to = target(y, z)
            if to is not None:
                route.append((y * SEQ_Z + z, to[0] * SEQ_Z + to[1]))
    return lax.ppermute(block, "seq", route)


def along_z(block, distance):
    return send(block, lambda y, z: (y, (z + distance) % SEQ_Z))


def along_y(block, distance):
    return send(block, lambda y, z: ((y + distance) % SEQ_Y, z))


def later_y(block, distance):
    return send(block, lambda y, z: (y + distance, z) if y + distance < SEQ_Y else None)


def across_z(block, bit):
    return send(block, lambda y, z: (y, z ^ bit))


SHORT = pl.CostEstimate(flops=5 * 10**8, bytes_accessed=2**16, transcendentals=0)
FULL = pl.CostEstimate(flops=2 * 10**9, bytes_accessed=2**16, transcendentals=0)


def prepare_kernel(key_ref, value_ref, out_ref, sems):
    copies = [
        pltpu.make_async_copy(source, out_ref.at[:, n * QDIM : (n + 1) * QDIM], sems.at[n])
        for n, source in enumerate((key_ref, value_ref))
    ]
    for copy in copies:
        copy.start()
    for copy in copies:
        copy.wait()


def prepare(key_rows, value_rows):
    return pl.pallas_call(
        prepare_kernel,
        out_shape=jax.ShapeDtypeStruct((SPAN, 2 * QDIM), jnp.bfloat16),
        in_specs=[ANY, ANY],
        out_specs=VMEM,
        scratch_shapes=[pltpu.SemaphoreType.DMA((2,))],
        cost_estimate=FULL,
        name="prepare",
    )(key_rows, value_rows)


def attend_kernel(segments, count, first, last, *refs):
    here_ref, query_ref = refs[0], refs[1]
    blocks = refs[2 : 2 + count]
    at = 2 + count + (0 if first else 2)
    max_ref, total_ref = refs[at : at + 2]
    wide_ref = refs[-1]
    heads = query_ref.shape[1] // QDIM
    rows = query_ref.shape[0]
    me = here_ref[0]
    my_y, my_z = lax.shift_right_logical(me, 3), lax.bitwise_and(me, SEQ_Z - 1)

    def source_of(place):
        up, along = place
        source_y = lax.bitwise_and(my_y + (up + SEQ_Y), SEQ_Y - 1)
        return source_y * SEQ_Z + lax.bitwise_and(my_z + (along + SEQ_Z), SEQ_Z - 1)

    wide_ref[:, QDIM:] = jnp.ones((wide_ref.shape[0], QDIM), jnp.bfloat16)

    def run(parts, masks, fresh):
        place = 0
        for which, offset, size, _ in parts:
            wide_ref[place : place + size, :QDIM] = blocks[which][offset : offset + size, QDIM:]
            place += size
        depth = place
        def first_product(head):
            query = query_ref[:, head * QDIM : (head + 1) * QDIM]
            pieces = []
            for which, offset, size, _ in parts:
                keys = blocks[which][offset : offset + size, :QDIM]
                pieces.append(
                    lax.dot_general(
                        query, keys, (((1,), (1,)), ((), ())), preferred_element_type=jnp.float32
                    )
                )
            if masks is not None:
                pieces = [
                    jnp.where(masks[at], piece, -1e30)
                    for at, piece in enumerate(
                        piece[:, n * SPAN : (n + 1) * SPAN]
                        for piece in pieces
                        for n in range(piece.shape[1] // SPAN)
                    )
                ]
            logits = pieces[0] if len(pieces) == 1 else jnp.concatenate(pieces, axis=1)
            return logits, jnp.max(logits, axis=1, keepdims=True)

        def second_product(head, logits, largest):
            if fresh:
                new = jnp.broadcast_to(largest, (rows, QDIM))
            else:
                old = max_ref[head]
                new = jnp.maximum(old, largest)
            max_ref[head] = new
            scaled = new * LOGIT_SCALE
            weights = jnp.exp2(logits * LOGIT_SCALE - scaled[:, :1]).astype(jnp.bfloat16)
            product = jnp.dot(
                weights, wide_ref[:depth, :], preferred_element_type=jnp.float32
            )
            if fresh:
                total_ref[head] = product
            else:
                rescale = jnp.exp2(old * LOGIT_SCALE - scaled)
                total_ref[head] = total_ref[head] * rescale[:, :1] + product

        following = first_product(0)
        for head in range(heads):
            current = following
            if head + 1 < heads:
                following = first_product(head + 1)
            second_product(head, *current)

    for kind, parts in segments:
        if kind == "own":
            ahead = (
                lax.broadcasted_iota(jnp.int32, (rows, SPAN), 1)
                - lax.broadcasted_iota(jnp.int32, (rows, SPAN), 0)
            )
            run(parts, [ahead <= 0], True)
            continue
        valid = [source_of(place) < me for part in parts for place in part[3]]
        some = functools.reduce(jnp.logical_or, valid)
        if kind == "row":
            pl.when(valid[0])(functools.partial(run, parts, None, False))
        else:
            pl.when(some)(functools.partial(run, parts, valid, False))

    if last:
        out_ref = refs[at + 2]
        for head in range(heads):
            total = total_ref[head]
            out_ref[:, head * QDIM : (head + 1) * QDIM] = (
                total[:, :QDIM] / total[:, QDIM:]
            ).astype(jnp.bfloat16)


def attend_step(queries, here, segments, carry, last):
    blocks, described = [], []
    deepest = 0
    for kind, segment in segments:
        parts = []
        for block, offset, size, places in segment:
            at = next((n for n, b in enumerate(blocks) if b is block), None)
            if at is None:
                at = len(blocks)
                blocks.append(block)
            parts.append((at, offset, size, places))
        described.append((kind, parts))
        deepest = max(deepest, sum(part[2] for part in parts))
    first = carry is None
    rows, width = queries.shape
    heads = width // QDIM
    carry_shapes = (
        jax.ShapeDtypeStruct((heads, rows, QDIM), jnp.float32),
        jax.ShapeDtypeStruct((heads, rows, 2 * QDIM), jnp.float32),
    )
    keys = sum(part[2] for _, parts in described for part in parts)
    operands = [here, queries, *blocks]
    aliases = {}
    if not first:
        aliases = {len(operands): 0, len(operands) + 1: 1}
        operands.extend(carry)
    out_shape = carry_shapes
    if last:
        out_shape = carry_shapes + (jax.ShapeDtypeStruct((rows, width), jnp.bfloat16),)
    outputs = pl.pallas_call(
        functools.partial(attend_kernel, described, len(blocks), first, last),
        out_shape=out_shape,
        in_specs=[SMEM] + [VMEM] * (len(operands) - 1),
        out_specs=(VMEM,) * len(out_shape),
        scratch_shapes=[pltpu.VMEM((deepest, 2 * QDIM), jnp.bfloat16)],
        input_output_aliases=aliases,
        compiler_params=pltpu.CompilerParams(vmem_limit_bytes=LIMIT),
        cost_estimate=SHORT,
        name="attend",
    )(*operands)
    return outputs[2] if last else outputs


def spread(columns, pair):
    lanes = lax.broadcasted_iota(jnp.int32, (columns.shape[0], 128), 1)
    return jnp.where(lanes < 64, columns[:, 2 * pair : 2 * pair + 1], columns[:, 2 * pair + 1 : 2 * pair + 2])


def triangle(rows):
    down = lax.broadcasted_iota(jnp.int32, (rows, rows), 0)
    along = lax.broadcasted_iota(jnp.int32, (rows, rows), 1)
    return down >= along


def state_kernel(
    x_in, b_in, c_in, decay_in, state_ref, fall_ref, columns_ref, x_ref, b_ref, c_ref, decay_ref, scaled_ref, sems
):
    copies = [
        pltpu.make_async_copy(source, target, sems.at[n])
        for n, (source, target) in enumerate(
            ((decay_in, decay_ref), (x_in, x_ref), (b_in, b_ref), (c_in, c_ref))
        )
    ]
    for copy in copies:
        copy.start()
    for copy in copies:
        copy.wait()
    rows = x_ref.shape[0]
    lower = triangle(rows).astype(jnp.float32)
    columns = lax.dot_general(
        lower, decay_ref[...], (((1,), (1,)), ((), ())), precision=HIGH,
        preferred_element_type=jnp.float32,
    )
    columns_ref[...] = columns
    total = columns[rows - 1 : rows, :]
    remaining = jnp.exp(total - columns)
    fall = jnp.broadcast_to(jnp.exp(total), (8, total.shape[1]))
    for pair in range(x_ref.shape[1] // 128):
        at = slice(pair * 128, (pair + 1) * 128)
        scaled_ref[:, at] = (x_ref[:, at].astype(jnp.float32) * spread(remaining, pair)).astype(jnp.bfloat16)
        fall_ref[:, at] = spread(fall, pair)
    state_ref[...] = lax.dot_general(
        b_ref[...], scaled_ref[...], (((0,), (0,)), ((), ())), preferred_element_type=jnp.float32
    )


def block_states(x, b, c, decay):
    rows, width = x.shape
    heads = decay.shape[0]
    return pl.pallas_call(
        state_kernel,
        out_shape=(
            jax.ShapeDtypeStruct((STATE, width), jnp.float32),
            jax.ShapeDtypeStruct((8, width), jnp.float32),
            jax.ShapeDtypeStruct((rows, heads), jnp.float32),
            jax.ShapeDtypeStruct(x.shape, x.dtype),
            jax.ShapeDtypeStruct(b.shape, b.dtype),
            jax.ShapeDtypeStruct(c.shape, c.dtype),
            jax.ShapeDtypeStruct(decay.shape, decay.dtype),
        ),
        in_specs=[ANY] * 4,
        out_specs=(VMEM,) * 7,
        scratch_shapes=[pltpu.VMEM((rows, width), jnp.bfloat16), pltpu.SemaphoreType.DMA((4,))],
        compiler_params=pltpu.CompilerParams(vmem_limit_bytes=LIMIT),
        cost_estimate=FULL,
        name="states",
    )(x, b, c, decay)


def within_kernel(x_ref, b_ref, c_ref, columns_ref, decay_ref, skip_ref, out_ref):
    rows = x_ref.shape[0]
    causal = triangle(rows)
    scores = lax.dot_general(
        c_ref[...], b_ref[...], (((1,), (1,)), ((), ())), preferred_element_type=jnp.float32
    )
    scores = jnp.where(causal, scores, 0.0)
    upper = jnp.where(causal, 0.0, 1.0) + jnp.where(
        lax.broadcasted_iota(jnp.int32, (rows, rows), 0) == lax.broadcasted_iota(jnp.int32, (rows, rows), 1), 1.0, 0.0
    )
    across = lax.dot_general(
        decay_ref[...], upper, (((1,), (0,)), ((), ())), precision=HIGH,
        preferred_element_type=jnp.float32,
    )
    columns = columns_ref[...]
    lanes = lax.broadcasted_iota(jnp.int32, (rows, 128), 1)
    for pair in range(x_ref.shape[1] // 128):
        at = slice(pair * 128, (pair + 1) * 128)
        x = x_ref[:, at]
        total = None
        for side in range(2):
            head = 2 * pair + side
            gap = jnp.minimum(columns[:, head : head + 1] - across[head : head + 1, :], 0.0)
            weights = (scores * jnp.exp(gap)).astype(jnp.bfloat16)
            mine = lanes < 64 if side == 0 else lanes >= 64
            product = jnp.dot(
                weights, jnp.where(mine, x, jnp.zeros_like(x)), preferred_element_type=jnp.float32
            )
            total = product if total is None else total + product
        out_ref[:, at] = total + skip_ref[:, at] * x.astype(jnp.float32)


def within_blocks(x, b, c, columns, decay, skip):
    rows, width = x.shape
    return pl.pallas_call(
        within_kernel,
        out_shape=jax.ShapeDtypeStruct((rows, width), jnp.float32),
        in_specs=[VMEM] * 6,
        out_specs=VMEM,
        compiler_params=pltpu.CompilerParams(vmem_limit_bytes=LIMIT),
        cost_estimate=FULL,
        name="within",
    )(x, b, c, columns, decay, skip)


def gate_kernel(within_ref, c_ref, carried_ref, columns_ref, gate_ref, gated_ref, squares_ref):
    grown = jnp.exp(columns_ref[...])
    total = None
    for pair in range(within_ref.shape[1] // 128):
        at = slice(pair * 128, (pair + 1) * 128)
        carried = jnp.dot(c_ref[...], carried_ref[:, at], preferred_element_type=jnp.float32)
        values = within_ref[:, at] + carried * spread(grown, pair)
        gate = gate_ref[:, at].astype(jnp.float32)
        gated = values * (gate / (1.0 + jnp.exp(-gate)))
        gated_ref[:, at] = gated
        total = gated * gated if total is None else total + gated * gated
    squares_ref[...] = lax.dot_general(
        jnp.ones((8, 128), jnp.float32), total, (((1,), (1,)), ((), ())), precision=HIGH,
        preferred_element_type=jnp.float32,
    )


def gate_values(within, c, carried, columns, gate):
    rows, width = within.shape
    return pl.pallas_call(
        gate_kernel,
        out_shape=(
            jax.ShapeDtypeStruct((rows, width), jnp.float32),
            jax.ShapeDtypeStruct((8, rows), jnp.float32),
        ),
        in_specs=[VMEM] * 5,
        out_specs=(VMEM, VMEM),
        compiler_params=pltpu.CompilerParams(vmem_limit_bytes=LIMIT),
        cost_estimate=FULL,
        name="gating",
    )(within, c, carried, columns, gate)


def norm_kernel(full_width, gated_ref, squares_ref, gain_ref, out_ref):
    total = lax.dot_general(
        squares_ref[...], jnp.full((8, 128), 0.125, jnp.float32), (((0,), (0,)), ((), ())),
        precision=HIGH, preferred_element_type=jnp.float32,
    )
    factor = lax.rsqrt(total * (1.0 / full_width) + EPSILON)
    for pair in range(gated_ref.shape[1] // 128):
        at = slice(pair * 128, (pair + 1) * 128)
        out_ref[:, at] = (gated_ref[:, at] * factor * gain_ref[:, at]).astype(jnp.bfloat16)


def normalize(gated, squares, gain, full_width):
    rows, width = gated.shape
    return pl.pallas_call(
        functools.partial(norm_kernel, full_width),
        out_shape=jax.ShapeDtypeStruct((rows, width), jnp.bfloat16),
        in_specs=[VMEM] * 3,
        out_specs=VMEM,
        compiler_params=pltpu.CompilerParams(vmem_limit_bytes=LIMIT),
        cost_estimate=FULL,
        name="normalize",
    )(gated, squares, gain)


def packed(state, fall):
    high = lax.reduce_precision(fall, 8, 7)
    return jnp.concatenate([state, high, fall - high], axis=0).astype(jnp.bfloat16)


def unpacked(message):
    wide = message.astype(jnp.float32)
    return wide[:STATE], wide[STATE : STATE + 8] + wide[STATE + 8 : STATE + 16]


def once(value, *others):
    return lax.optimization_barrier((value, *others))[0]


def entering_state(state, fall, me, needs, turns):
    kept = []
    needs, turns = iter(needs), iter(turns)
    for level in range(3):
        upper = (me >> level) & 1 == 1
        width = state.shape[1] // 2
        low, high = state[:, :width], state[:, width:]
        fall_low, fall_high = fall[:, :width], fall[:, width:]
        mine, mine_fall = jnp.where(upper, high, low), jnp.where(upper, fall_high, fall_low)
        message = packed(jnp.where(upper, low, high), jnp.where(upper, fall_low, fall_high))
        received = across_z(once(message, *next(needs)), 1 << level)
        turn = next(turns)
        if callable(turn):
            turn = turn(received)
        theirs, their_fall = unpacked(once(received, *turn))
        before, after = jnp.where(upper, theirs, mine), jnp.where(upper, mine, theirs)
        before_fall = jnp.where(upper, their_fall, mine_fall)
        after_fall = jnp.where(upper, mine_fall, their_fall)
        kept.append((upper, before, before_fall))
        state = after_fall[:1] * before + after
        fall = before_fall * after_fall
    message = once(packed(state, fall), *next(needs))
    moved = [along_y(message, 1), along_y(message, -1), along_y(message, 2)]
    moved = lax.optimization_barrier((*moved, *next(turns)))[:3]
    (one, one_fall), (three, _), (two, two_fall) = (unpacked(block) for block in moved)
    y_at = lax.shift_right_logical(me, 3)
    one, two, three = (jnp.where(y_at >= n, block, 0.0) for n, block in ((1, one), (2, two), (3, three)))
    entering = one + one_fall[:1] * (two + two_fall[:1] * three)
    for level in reversed(range(3)):
        upper, before, before_fall = kept[level]
        second = before_fall[:1] * entering + before
        mine = jnp.where(upper, second, entering)
        other = jnp.where(upper, entering, second).astype(jnp.bfloat16)
        received = once(across_z(once(other, *next(needs)), 1 << level), *next(turns)).astype(jnp.float32)
        entering = jnp.where(
            upper,
            jnp.concatenate([received, mine], axis=1),
            jnp.concatenate([mine, received], axis=1),
        )
    return entering.astype(jnp.bfloat16)


def sum_over_heads(squares, turns):
    devices = lax.axis_size("head")

    def moved(block, bits):
        return lax.ppermute(block, "head", [(i, i ^ bits) for i in range(devices)])

    squares = squares + once(moved(squares, 1), *turns[0])
    others = [moved(squares, 2 * n) for n in range(1, devices // 2)]
    return sum(lax.optimization_barrier((*others, *turns[1]))[: len(others)], squares)


def body(
    mixer_input, gate_input, input_b, input_c, log_decay, skip_gain, norm_gain, queries, key_rows, value_rows
):
    me = lax.axis_index("seq").astype(jnp.int32)
    here = me[None]
    head_width = mixer_input.shape[1] // skip_gain.shape[0]
    full_width = mixer_input.shape[1] * lax.axis_size("head")

    own = prepare(key_rows, value_rows)
    state, fall, columns, x, b, c, decay = block_states(mixer_input, input_b, input_c, log_decay)

    up, down = [own], [own]
    for step in range(4):
        up.append(along_z(up[-1], 1))
        if step < 3:
            down.append(along_z(down[-1], -1))
    parts = [[(0, own), (-1, up[1]), (1, down[1]), (-2, up[2]), (2, down[2])], [(-3, up[3]), (3, down[3]), (-4, up[4])]]
    packs = [jnp.concatenate([block for _, block in part], axis=0) for part in parts]
    above = [along_y(pack, 1) for pack in packs]
    below = [along_y(pack, -1) for pack in packs]
    across = [along_y(above[0], 1), along_y(below[1], -1)]

    def from_row(which, blocks, row, start=0, stop=None):
        places = [(row, z) for z, _ in parts[which]][start:stop]
        return ("row", [(blocks[which], start * SPAN, len(places) * SPAN, places)])

    withins = []

    def compute_within(received):
        spread_skip = jnp.repeat(skip_gain, head_width)[None, :]
        withins.append(within_blocks(once(x, received), b, c, columns, decay, spread_skip))
        return []

    def near(part):
        return ("blocks", [(block, 0, SPAN, [(0, z)]) for z, block in part])

    steps = [
        [("own", [(once(own, up[3], down[3]), 0, SPAN, [(0, 0)])]), near(parts[0][1:] + parts[1][:2])],
        [near(parts[1][2:]), from_row(0, above, -1)],
        [from_row(0, below, 1)],
        [from_row(1, above, -1), from_row(1, below, 1)],
        [from_row(1, across, 2)],
        [from_row(0, across, 2, 0, 3)],
        [from_row(0, across, 2, 3, 5)],
    ]
    carry, done = None, []
    for at, segments in enumerate(steps):
        carry = attend_step(queries, here, segments, carry, at == len(steps) - 1)
        done.append(carry if at == len(steps) - 1 else carry[0])
    needs = [[], [up[2], down[2]], [up[3], down[3]], [up[4], above[0], below[0]], [], [above[1], below[1]], []]
    turns = [compute_within, withins] + [[done[n]] for n in range(5)]
    carried = entering_state(state, fall, me, needs, turns)
    attended = done[-1]

    gated, squares = gate_values(withins[0], c, carried, columns, gate_input)
    squares = sum_over_heads(squares, [[done[5]], [done[6]]])
    mixer_output = normalize(gated, squares, norm_gain[None, :], full_width)
    return (mixer_output, attended)


def solution(mesh):
    return jax.shard_map(
        body,
        mesh=mesh,
        in_specs=(
            P("seq", "head"),
            P("seq", "head"),
            P("seq", "head"),
            P("seq", "head"),
            P("head", "seq"),
            P("head"),
            P("head"),
            P("seq", "head"),
            P("seq", "head"),
            P("seq", "head"),
        ),
        out_specs=(P("seq", "head"), P("seq", "head")),
        check_vma=False,
    )
```

```python
import functools
import math

import jax
import jax.numpy as jnp
from jax import lax
from jax.experimental import pallas as pl
from jax.experimental.pallas import tpu as pltpu
from jax.sharding import PartitionSpec as P

STATE = 128
QDIM = 128
SPAN = 256
EPSILON = 1e-05
SEQ_Y, SEQ_Z = 4, 8
LOGIT_SCALE = QDIM ** (-0.5) * math.log2(math.e)
HIGH = lax.Precision.HIGHEST
VMEM = pl.BlockSpec(memory_space=pltpu.VMEM)
ANY = pl.BlockSpec(memory_space=pl.ANY)
SMEM = pl.BlockSpec(memory_space=pltpu.SMEM)
LIMIT = 40 * 2**20


def send(block, target):
    route = []
    for y in range(SEQ_Y):
        for z in range(SEQ_Z):
            to = target(y, z)
            if to is not None:
                route.append((y * SEQ_Z + z, to[0] * SEQ_Z + to[1]))
    return lax.ppermute(block, "seq", route)


def along_z(block, distance):
    return send(block, lambda y, z: (y, (z + distance) % SEQ_Z))


def along_y(block, distance):
    return send(block, lambda y, z: ((y + distance) % SEQ_Y, z))


def later_y(block, distance):
    return send(block, lambda y, z: (y + distance, z) if y + distance < SEQ_Y else None)


def across_z(block, bit):
    return send(block, lambda y, z: (y, z ^ bit))


SHORT = pl.CostEstimate(flops=5 * 10**8, bytes_accessed=2**16, transcendentals=0)
FULL = pl.CostEstimate(flops=2 * 10**9, bytes_accessed=2**16, transcendentals=0)


def prepare_kernel(key_ref, value_ref, out_ref, sems):
    copies = [
        pltpu.make_async_copy(source, out_ref.at[:, n * QDIM : (n + 1) * QDIM], sems.at[n])
        for n, source in enumerate((key_ref, value_ref))
    ]
    for copy in copies:
        copy.start()
    for copy in copies:
        copy.wait()


def prepare(key_rows, value_rows):
    return pl.pallas_call(
        prepare_kernel,
        out_shape=jax.ShapeDtypeStruct((SPAN, 2 * QDIM), jnp.bfloat16),
        in_specs=[ANY, ANY],
        out_specs=VMEM,
        scratch_shapes=[pltpu.SemaphoreType.DMA((2,))],
        cost_estimate=FULL,
        name="prepare",
    )(key_rows, value_rows)


def attend_kernel(segments, count, first, last, *refs):
    here_ref, query_ref = refs[0], refs[1]
    blocks = refs[2 : 2 + count]
    at = 2 + count
    old_total_ref = None
    if not first:
        old_total_ref = refs[at + 1]
        at += 2
    max_ref, total_ref = refs[at : at + 2]
    wide_ref, excess_ref = refs[-2:]
    heads = query_ref.shape[1] // QDIM
    rows = query_ref.shape[0]
    me = here_ref[0]
    my_y, my_z = lax.shift_right_logical(me, 3), lax.bitwise_and(me, SEQ_Z - 1)

    def source_of(place):
        up, along = place
        source_y = lax.bitwise_and(my_y + (up + SEQ_Y), SEQ_Y - 1)
        return source_y * SEQ_Z + lax.bitwise_and(my_z + (along + SEQ_Z), SEQ_Z - 1)

    wide_ref[:, QDIM:] = jnp.ones((wide_ref.shape[0], QDIM), jnp.bfloat16)
    excess_ref[...] = jnp.zeros(excess_ref.shape, jnp.float32)

    def take_values(parts):
        place = 0
        for which, offset, size, _ in parts:
            wide_ref[place : place + size, :QDIM] = blocks[which][offset : offset + size, QDIM:]
            place += size
        return place

    def first_product(head, parts, masks):
        if isinstance(head, int):
            query = query_ref[:, head * QDIM : (head + 1) * QDIM]
        else:
            query = query_ref[:, pl.ds(pl.multiple_of(head * QDIM, QDIM), QDIM)]
        pieces = []
        for which, offset, size, _ in parts:
            keys = blocks[which][offset : offset + size, :QDIM]
            pieces.append(
                lax.dot_general(query, keys, (((1,), (1,)), ((), ())), preferred_element_type=jnp.float32)
            )
        if masks is not None:
            pieces = [
                jnp.where(masks[at], piece, -1e30)
                for at, piece in enumerate(
                    piece[:, n * SPAN : (n + 1) * SPAN]
                    for piece in pieces
                    for n in range(piece.shape[1] // SPAN)
                )
            ]
        return pieces[0] if len(pieces) == 1 else jnp.concatenate(pieces, axis=1)

    def weigh(logits, largest):
        return jnp.exp2(logits * LOGIT_SCALE - (largest * LOGIT_SCALE)[:, :1]).astype(jnp.bfloat16)

    def begin(head, parts, masks, depth):
        logits = first_product(head, parts, masks)
        largest = jnp.broadcast_to(jnp.max(logits, axis=1, keepdims=True), (rows, QDIM))
        max_ref[head] = largest
        total_ref[head] = jnp.dot(
            weigh(logits, largest), wide_ref[:depth, :], preferred_element_type=jnp.float32
        )

    def quick(parts, masks, base_ref):
        depth = take_values(parts)
        excess = None
        following = first_product(0, parts, masks)
        for head in range(heads):
            logits = following
            if head + 1 < heads:
                following = first_product(head + 1, parts, masks)
            largest = max_ref[head]
            total_ref[head] = base_ref[head] + jnp.dot(
                weigh(logits, largest), wide_ref[:depth, :], preferred_element_type=jnp.float32
            )
            columns = [logits[:, n * QDIM : (n + 1) * QDIM] for n in range(depth // QDIM)]
            over = functools.reduce(jnp.maximum, columns) - largest
            excess = over if excess is None else jnp.maximum(excess, over)
        excess_ref[...] = jnp.maximum(excess_ref[...], excess)

    def careful(parts, masks):
        depth = take_values(parts)

        def one_head(head, nothing):
            logits = first_product(head, parts, masks)
            old = max_ref[head]
            new = jnp.maximum(old, jnp.max(logits, axis=1, keepdims=True))
            max_ref[head] = new
            rescale = jnp.exp2(old * LOGIT_SCALE - new * LOGIT_SCALE)
            total_ref[head] = total_ref[head] * rescale[:, :1] + jnp.dot(
                weigh(logits, new), wide_ref[:depth, :], preferred_element_type=jnp.float32
            )
            return nothing

        lax.fori_loop(0, heads, one_head, 0)

    ahead = lax.broadcasted_iota(jnp.int32, (rows, SPAN), 1) - lax.broadcasted_iota(jnp.int32, (rows, SPAN), 0)
    work = []
    for kind, parts in segments:
        valid = [source_of(place) < me for part in parts for place in part[3]]
        if kind == "own":
            work.append((None, parts, [ahead <= 0]))
        elif kind == "row":
            work.append((valid[0], parts, None))
        else:
            work.append((functools.reduce(jnp.logical_or, valid), parts, valid))

    for n, (condition, parts, masks) in enumerate(work):
        if condition is None:
            depth = take_values(parts)
            for head in range(heads):
                begin(head, parts, masks, depth)
            continue
        base_ref = total_ref
        if n == 0:
            base_ref = old_total_ref

            @pl.when(jnp.logical_not(condition))
            def _():
                total_ref[...] = old_total_ref[...]

        pl.when(condition)(functools.partial(quick, parts, masks, base_ref))

    @pl.when(jnp.max(excess_ref[...]) * LOGIT_SCALE > 64.0)
    def _():
        if not first:
            total_ref[...] = old_total_ref[...]
        for condition, parts, masks in work:
            if condition is None:
                depth = take_values(parts)
                for head in range(heads):
                    begin(head, parts, masks, depth)
            else:
                pl.when(condition)(functools.partial(careful, parts, masks))

    if last:
        out_ref = refs[at + 2]
        for head in range(heads):
            total = total_ref[head]
            out_ref[:, head * QDIM : (head + 1) * QDIM] = (
                total[:, :QDIM] / total[:, QDIM:]
            ).astype(jnp.bfloat16)


def attend_step(queries, here, segments, carry, last):
    blocks, described = [], []
    deepest = 0
    for kind, segment in segments:
        parts = []
        for block, offset, size, places in segment:
            at = next((n for n, b in enumerate(blocks) if b is block), None)
            if at is None:
                at = len(blocks)
                blocks.append(block)
            parts.append((at, offset, size, places))
        described.append((kind, parts))
        deepest = max(deepest, sum(part[2] for part in parts))
    first = carry is None
    rows, width = queries.shape
    heads = width // QDIM
    carry_shapes = (
        jax.ShapeDtypeStruct((heads, rows, QDIM), jnp.float32),
        jax.ShapeDtypeStruct((heads, rows, 2 * QDIM), jnp.float32),
    )
    keys = sum(part[2] for _, parts in described for part in parts)
    operands = [here, queries, *blocks]
    aliases = {}
    if not first:
        aliases = {len(operands): 0}
        operands.extend(carry)
    out_shape = carry_shapes
    if last:
        out_shape = carry_shapes + (jax.ShapeDtypeStruct((rows, width), jnp.bfloat16),)
    outputs = pl.pallas_call(
        functools.partial(attend_kernel, described, len(blocks), first, last),
        out_shape=out_shape,
        in_specs=[SMEM] + [VMEM] * (len(operands) - 1),
        out_specs=(VMEM,) * len(out_shape),
        scratch_shapes=[
            pltpu.VMEM((deepest, 2 * QDIM), jnp.bfloat16),
            pltpu.VMEM((rows, QDIM), jnp.float32),
        ],
        input_output_aliases=aliases,
        compiler_params=pltpu.CompilerParams(vmem_limit_bytes=LIMIT),
        cost_estimate=SHORT,
        name="attend",
    )(*operands)
    return outputs[2] if last else outputs


def spread(columns, pair):
    lanes = lax.broadcasted_iota(jnp.int32, (columns.shape[0], 128), 1)
    return jnp.where(lanes < 64, columns[:, 2 * pair : 2 * pair + 1], columns[:, 2 * pair + 1 : 2 * pair + 2])


def triangle(rows):
    down = lax.broadcasted_iota(jnp.int32, (rows, rows), 0)
    along = lax.broadcasted_iota(jnp.int32, (rows, rows), 1)
    return down >= along


def state_kernel(
    x_in, b_in, c_in, decay_in, state_ref, fall_ref, columns_ref, x_ref, b_ref, c_ref, decay_ref, scaled_ref, sems
):
    copies = [
        pltpu.make_async_copy(source, target, sems.at[n])
        for n, (source, target) in enumerate(
            ((decay_in, decay_ref), (x_in, x_ref), (b_in, b_ref), (c_in, c_ref))
        )
    ]
    for copy in copies:
        copy.start()
    for copy in copies:
        copy.wait()
    rows = x_ref.shape[0]
    lower = triangle(rows).astype(jnp.float32)
    columns = lax.dot_general(
        lower, decay_ref[...], (((1,), (1,)), ((), ())), precision=HIGH,
        preferred_element_type=jnp.float32,
    )
    columns_ref[...] = columns
    total = columns[rows - 1 : rows, :]
    remaining = jnp.exp(total - columns)
    fall = jnp.broadcast_to(jnp.exp(total), (8, total.shape[1]))
    for pair in range(x_ref.shape[1] // 128):
        at = slice(pair * 128, (pair + 1) * 128)
        scaled_ref[:, at] = (x_ref[:, at].astype(jnp.float32) * spread(remaining, pair)).astype(jnp.bfloat16)
        fall_ref[:, at] = spread(fall, pair)
    state_ref[...] = lax.dot_general(
        b_ref[...], scaled_ref[...], (((0,), (0,)), ((), ())), preferred_element_type=jnp.float32
    )


def block_states(x, b, c, decay):
    rows, width = x.shape
    heads = decay.shape[0]
    return pl.pallas_call(
        state_kernel,
        out_shape=(
            jax.ShapeDtypeStruct((STATE, width), jnp.float32),
            jax.ShapeDtypeStruct((8, width), jnp.float32),
            jax.ShapeDtypeStruct((rows, heads), jnp.float32),
            jax.ShapeDtypeStruct(x.shape, x.dtype),
            jax.ShapeDtypeStruct(b.shape, b.dtype),
            jax.ShapeDtypeStruct(c.shape, c.dtype),
            jax.ShapeDtypeStruct(decay.shape, decay.dtype),
        ),
        in_specs=[ANY] * 4,
        out_specs=(VMEM,) * 7,
        scratch_shapes=[pltpu.VMEM((rows, width), jnp.bfloat16), pltpu.SemaphoreType.DMA((4,))],
        compiler_params=pltpu.CompilerParams(vmem_limit_bytes=LIMIT),
        cost_estimate=FULL,
        name="states",
    )(x, b, c, decay)


def within_kernel(x_ref, b_ref, c_ref, columns_ref, decay_ref, skip_ref, out_ref):
    rows = x_ref.shape[0]
    causal = triangle(rows)
    scores = lax.dot_general(
        c_ref[...], b_ref[...], (((1,), (1,)), ((), ())), preferred_element_type=jnp.float32
    )
    scores = jnp.where(causal, scores, 0.0)
    upper = jnp.where(causal, 0.0, 1.0) + jnp.where(
        lax.broadcasted_iota(jnp.int32, (rows, rows), 0) == lax.broadcasted_iota(jnp.int32, (rows, rows), 1), 1.0, 0.0
    )
    across = lax.dot_general(
        decay_ref[...], upper, (((1,), (0,)), ((), ())), precision=HIGH,
        preferred_element_type=jnp.float32,
    )
    columns = columns_ref[...]
    lanes = lax.broadcasted_iota(jnp.int32, (rows, 128), 1)
    for pair in range(x_ref.shape[1] // 128):
        at = slice(pair * 128, (pair + 1) * 128)
        x = x_ref[:, at]
        total = None
        for side in range(2):
            head = 2 * pair + side
            gap = jnp.minimum(columns[:, head : head + 1] - across[head : head + 1, :], 0.0)
            weights = (scores * jnp.exp(gap)).astype(jnp.bfloat16)
            mine = lanes < 64 if side == 0 else lanes >= 64
            product = jnp.dot(
                weights, jnp.where(mine, x, jnp.zeros_like(x)), preferred_element_type=jnp.float32
            )
            total = product if total is None else total + product
        out_ref[:, at] = total + skip_ref[:, at] * x.astype(jnp.float32)


def within_blocks(x, b, c, columns, decay, skip):
    rows, width = x.shape
    return pl.pallas_call(
        within_kernel,
        out_shape=jax.ShapeDtypeStruct((rows, width), jnp.float32),
        in_specs=[VMEM] * 6,
        out_specs=VMEM,
        compiler_params=pltpu.CompilerParams(vmem_limit_bytes=LIMIT),
        cost_estimate=FULL,
        name="within",
    )(x, b, c, columns, decay, skip)


def gate_kernel(within_ref, c_ref, carried_ref, columns_ref, gate_ref, gated_ref, squares_ref):
    grown = jnp.exp(columns_ref[...])
    total = None
    for pair in range(within_ref.shape[1] // 128):
        at = slice(pair * 128, (pair + 1) * 128)
        carried = jnp.dot(c_ref[...], carried_ref[:, at], preferred_element_type=jnp.float32)
        values = within_ref[:, at] + carried * spread(grown, pair)
        gate = gate_ref[:, at].astype(jnp.float32)
        gated = values * (gate / (1.0 + jnp.exp(-gate)))
        gated_ref[:, at] = gated
        total = gated * gated if total is None else total + gated * gated
    squares_ref[...] = lax.dot_general(
        jnp.ones((8, 128), jnp.float32), total, (((1,), (1,)), ((), ())), precision=HIGH,
        preferred_element_type=jnp.float32,
    )


def gate_values(within, c, carried, columns, gate):
    rows, width = within.shape
    return pl.pallas_call(
        gate_kernel,
        out_shape=(
            jax.ShapeDtypeStruct((rows, width), jnp.float32),
            jax.ShapeDtypeStruct((8, rows), jnp.float32),
        ),
        in_specs=[VMEM] * 5,
        out_specs=(VMEM, VMEM),
        compiler_params=pltpu.CompilerParams(vmem_limit_bytes=LIMIT),
        cost_estimate=FULL,
        name="gating",
    )(within, c, carried, columns, gate)


def norm_kernel(full_width, gated_ref, squares_ref, gain_ref, out_ref):
    total = lax.dot_general(
        squares_ref[...], jnp.full((8, 128), 0.125, jnp.float32), (((0,), (0,)), ((), ())),
        precision=HIGH, preferred_element_type=jnp.float32,
    )
    factor = lax.rsqrt(total * (1.0 / full_width) + EPSILON)
    for pair in range(gated_ref.shape[1] // 128):
        at = slice(pair * 128, (pair + 1) * 128)
        out_ref[:, at] = (gated_ref[:, at] * factor * gain_ref[:, at]).astype(jnp.bfloat16)


def normalize(gated, squares, gain, full_width):
    rows, width = gated.shape
    return pl.pallas_call(
        functools.partial(norm_kernel, full_width),
        out_shape=jax.ShapeDtypeStruct((rows, width), jnp.bfloat16),
        in_specs=[VMEM] * 3,
        out_specs=VMEM,
        compiler_params=pltpu.CompilerParams(vmem_limit_bytes=LIMIT),
        cost_estimate=FULL,
        name="normalize",
    )(gated, squares, gain)


def packed(state, fall):
    high = lax.reduce_precision(fall, 8, 7)
    return jnp.concatenate([state, high, fall - high], axis=0).astype(jnp.bfloat16)


def unpacked(message):
    wide = message.astype(jnp.float32)
    return wide[:STATE], wide[STATE : STATE + 8] + wide[STATE + 8 : STATE + 16]


def once(value, *others):
    return lax.optimization_barrier((value, *others))[0]


def entering_state(state, fall, me, needs, turns):
    kept = []
    needs, turns = iter(needs), iter(turns)
    for level in range(3):
        upper = (me >> level) & 1 == 1
        width = state.shape[1] // 2
        low, high = state[:, :width], state[:, width:]
        fall_low, fall_high = fall[:, :width], fall[:, width:]
        mine, mine_fall = jnp.where(upper, high, low), jnp.where(upper, fall_high, fall_low)
        message = packed(jnp.where(upper, low, high), jnp.where(upper, fall_low, fall_high))
        received = across_z(once(message, *next(needs)), 1 << level)
        turn = next(turns)
        if callable(turn):
            turn = turn(received)
        theirs, their_fall = unpacked(once(received, *turn))
        before, after = jnp.where(upper, theirs, mine), jnp.where(upper, mine, theirs)
        before_fall = jnp.where(upper, their_fall, mine_fall)
        after_fall = jnp.where(upper, mine_fall, their_fall)
        kept.append((upper, before, before_fall))
        state = after_fall[:1] * before + after
        fall = before_fall * after_fall
    message = once(packed(state, fall), *next(needs))
    moved = [along_y(message, 1), along_y(message, -1), along_y(message, 2)]
    moved = lax.optimization_barrier((*moved, *next(turns)))[:3]
    (one, one_fall), (three, _), (two, two_fall) = (unpacked(block) for block in moved)
    y_at = lax.shift_right_logical(me, 3)
    one, two, three = (jnp.where(y_at >= n, block, 0.0) for n, block in ((1, one), (2, two), (3, three)))
    entering = one + one_fall[:1] * (two + two_fall[:1] * three)
    for level in reversed(range(3)):
        upper, before, before_fall = kept[level]
        second = before_fall[:1] * entering + before
        mine = jnp.where(upper, second, entering)
        other = jnp.where(upper, entering, second).astype(jnp.bfloat16)
        received = once(across_z(once(other, *next(needs)), 1 << level), *next(turns)).astype(jnp.float32)
        entering = jnp.where(
            upper,
            jnp.concatenate([received, mine], axis=1),
            jnp.concatenate([mine, received], axis=1),
        )
    return entering.astype(jnp.bfloat16)


def sum_over_heads(squares, turns):
    devices = lax.axis_size("head")

    def moved(block, bits):
        return lax.ppermute(block, "head", [(i, i ^ bits) for i in range(devices)])

    squares = squares + once(moved(squares, 1), *turns[0])
    others = [moved(squares, 2 * n) for n in range(1, devices // 2)]
    return sum(lax.optimization_barrier((*others, *turns[1]))[: len(others)], squares)


def body(
    mixer_input, gate_input, input_b, input_c, log_decay, skip_gain, norm_gain, queries, key_rows, value_rows
):
    me = lax.axis_index("seq").astype(jnp.int32)
    here = me[None]
    head_width = mixer_input.shape[1] // skip_gain.shape[0]
    full_width = mixer_input.shape[1] * lax.axis_size("head")

    own = prepare(key_rows, value_rows)
    state, fall, columns, x, b, c, decay = block_states(mixer_input, input_b, input_c, log_decay)

    up, down = [own], [own]
    for step in range(4):
        up.append(along_z(up[-1], 1))
        if step < 3:
            down.append(along_z(down[-1], -1))
    parts = [[(0, own), (-1, up[1]), (1, down[1]), (-2, up[2]), (2, down[2])], [(-3, up[3]), (3, down[3]), (-4, up[4])]]
    packs = [jnp.concatenate([block for _, block in part], axis=0) for part in parts]
    above = [along_y(pack, 1) for pack in packs]
    below = [along_y(pack, -1) for pack in packs]
    across = [along_y(above[0], 1), along_y(below[1], -1)]

    def from_row(which, blocks, row, start=0, stop=None):
        places = [(row, z) for z, _ in parts[which]][start:stop]
        return ("row", [(blocks[which], start * SPAN, len(places) * SPAN, places)])

    withins = []

    def compute_within(received):
        spread_skip = jnp.repeat(skip_gain, head_width)[None, :]
        withins.append(within_blocks(once(x, received), b, c, columns, decay, spread_skip))
        needs[1].append(withins[0])
        return []

    def near(part):
        return ("blocks", [(block, 0, SPAN, [(0, z)]) for z, block in part])

    steps = [
        [("own", [(own, 0, SPAN, [(0, 0)])]), near(parts[0][1:])],
        [near(parts[1][:2])],
        [near(parts[1][2:]), from_row(0, above, -1)],
        [from_row(0, below, 1)],
        [from_row(1, above, -1), from_row(1, below, 1)],
        [from_row(1, across, 2)],
        [from_row(0, across, 2, 0, 3)],
        [from_row(0, across, 2, 3, 5)],
    ]
    carry, done = None, []
    for at, segments in enumerate(steps):
        carry = attend_step(queries, here, segments, carry, at == len(steps) - 1)
        done.append(carry if at == len(steps) - 1 else carry[0])
    needs = [[], [up[2], down[2]], [up[3], down[3]], [up[4], above[0], below[0]], [], [above[1], below[1]], []]
    turns = [compute_within] + [[done[n]] for n in range(6)]
    carried = entering_state(state, fall, me, needs, turns)
    attended = done[-1]

    gated, squares = gate_values(withins[0], c, carried, columns, gate_input)
    squares = sum_over_heads(squares, [[done[6]], [done[7]]])
    mixer_output = normalize(gated, squares, norm_gain[None, :], full_width)
    return (mixer_output, attended)


def solution(mesh):
    return jax.shard_map(
        body,
        mesh=mesh,
        in_specs=(
            P("seq", "head"),
            P("seq", "head"),
            P("seq", "head"),
            P("seq", "head"),
            P("head", "seq"),
            P("head"),
            P("head"),
            P("seq", "head"),
            P("seq", "head"),
            P("seq", "head"),
        ),
        out_specs=(P("seq", "head"), P("seq", "head")),
        check_vma=False,
    )
```

```python
import functools
import math

import jax
import jax.numpy as jnp
from jax import lax
from jax.experimental import pallas as pl
from jax.experimental.pallas import tpu as pltpu
from jax.sharding import PartitionSpec as P

STATE = 128
QDIM = 128
SPAN = 256
EPSILON = 1e-05
SEQ_Y, SEQ_Z = 4, 8
LOGIT_SCALE = QDIM ** (-0.5) * math.log2(math.e)
HIGH = lax.Precision.HIGHEST
VMEM = pl.BlockSpec(memory_space=pltpu.VMEM)
ANY = pl.BlockSpec(memory_space=pl.ANY)
SMEM = pl.BlockSpec(memory_space=pltpu.SMEM)
LIMIT = 40 * 2**20


def send(block, target):
    route = []
    for y in range(SEQ_Y):
        for z in range(SEQ_Z):
            to = target(y, z)
            if to is not None:
                route.append((y * SEQ_Z + z, to[0] * SEQ_Z + to[1]))
    return lax.ppermute(block, "seq", route)


def along_z(block, distance):
    return send(block, lambda y, z: (y, (z + distance) % SEQ_Z))


def along_y(block, distance):
    return send(block, lambda y, z: ((y + distance) % SEQ_Y, z))


def later_y(block, distance):
    return send(block, lambda y, z: (y + distance, z) if y + distance < SEQ_Y else None)


def across_z(block, bit):
    return send(block, lambda y, z: (y, z ^ bit))


SHORT = pl.CostEstimate(flops=5 * 10**8, bytes_accessed=2**16, transcendentals=0)
FULL = pl.CostEstimate(flops=2 * 10**9, bytes_accessed=2**16, transcendentals=0)


def prepare_kernel(key_ref, value_ref, out_ref, sems):
    copies = [
        pltpu.make_async_copy(source, out_ref.at[:, n * QDIM : (n + 1) * QDIM], sems.at[n])
        for n, source in enumerate((key_ref, value_ref))
    ]
    for copy in copies:
        copy.start()
    for copy in copies:
        copy.wait()


def prepare(key_rows, value_rows):
    return pl.pallas_call(
        prepare_kernel,
        out_shape=jax.ShapeDtypeStruct((SPAN, 2 * QDIM), jnp.bfloat16),
        in_specs=[ANY, ANY],
        out_specs=VMEM,
        scratch_shapes=[pltpu.SemaphoreType.DMA((2,))],
        cost_estimate=FULL,
        name="prepare",
    )(key_rows, value_rows)


def attend_kernel(segments, count, first, last, *refs):
    here_ref, query_ref = refs[0], refs[1]
    blocks = refs[2 : 2 + count]
    at = 2 + count
    old_total_ref = None
    if not first:
        old_total_ref = refs[at + 1]
        at += 2
    max_ref, total_ref = refs[at : at + 2]
    wide_ref, excess_ref = refs[-2:]
    heads = query_ref.shape[1] // QDIM
    rows = query_ref.shape[0]
    me = here_ref[0]
    my_y, my_z = lax.shift_right_logical(me, 3), lax.bitwise_and(me, SEQ_Z - 1)

    def source_of(place):
        up, along = place
        source_y = lax.bitwise_and(my_y + (up + SEQ_Y), SEQ_Y - 1)
        return source_y * SEQ_Z + lax.bitwise_and(my_z + (along + SEQ_Z), SEQ_Z - 1)

    wide_ref[:, QDIM:] = jnp.ones((wide_ref.shape[0], QDIM), jnp.bfloat16)
    excess_ref[...] = jnp.zeros(excess_ref.shape, jnp.float32)

    def take_values(parts):
        place = 0
        for which, offset, size, _ in parts:
            wide_ref[place : place + size, :QDIM] = blocks[which][offset : offset + size, QDIM:]
            place += size
        return place

    def first_product(head, parts, masks):
        if isinstance(head, int):
            query = query_ref[:, head * QDIM : (head + 1) * QDIM]
        else:
            query = query_ref[:, pl.ds(pl.multiple_of(head * QDIM, QDIM), QDIM)]
        pieces = []
        for which, offset, size, _ in parts:
            keys = blocks[which][offset : offset + size, :QDIM]
            pieces.append(
                lax.dot_general(query, keys, (((1,), (1,)), ((), ())), preferred_element_type=jnp.float32)
            )
        if masks is not None:
            pieces = [
                jnp.where(masks[at], piece, -1e30)
                for at, piece in enumerate(
                    piece[:, n * SPAN : (n + 1) * SPAN]
                    for piece in pieces
                    for n in range(piece.shape[1] // SPAN)
                )
            ]
        return pieces[0] if len(pieces) == 1 else jnp.concatenate(pieces, axis=1)

    def weigh(logits, largest):
        return jnp.exp2(logits * LOGIT_SCALE - (largest * LOGIT_SCALE)[:, :1]).astype(jnp.bfloat16)

    def begin(head, parts, masks, depth):
        logits = first_product(head, parts, masks)
        largest = jnp.broadcast_to(jnp.max(logits, axis=1, keepdims=True), (rows, QDIM))
        max_ref[head] = largest
        total_ref[head] = jnp.dot(
            weigh(logits, largest), wide_ref[:depth, :], preferred_element_type=jnp.float32
        )

    def quick(parts, masks, base_ref):
        depth = take_values(parts)
        excess = None
        following = first_product(0, parts, masks)
        for head in range(heads):
            logits = following
            if head + 1 < heads:
                following = first_product(head + 1, parts, masks)
            largest = max_ref[head]
            total_ref[head] = base_ref[head] + jnp.dot(
                weigh(logits, largest), wide_ref[:depth, :], preferred_element_type=jnp.float32
            )
            columns = [logits[:, n * QDIM : (n + 1) * QDIM] for n in range(depth // QDIM)]
            over = functools.reduce(jnp.maximum, columns) - largest
            excess = over if excess is None else jnp.maximum(excess, over)
        excess_ref[...] = jnp.maximum(excess_ref[...], excess)

    def careful(parts, masks):
        depth = take_values(parts)

        def one_head(head, nothing):
            logits = first_product(head, parts, masks)
            old = max_ref[head]
            new = jnp.maximum(old, jnp.max(logits, axis=1, keepdims=True))
            max_ref[head] = new
            rescale = jnp.exp2(old * LOGIT_SCALE - new * LOGIT_SCALE)
            total_ref[head] = total_ref[head] * rescale[:, :1] + jnp.dot(
                weigh(logits, new), wide_ref[:depth, :], preferred_element_type=jnp.float32
            )
            return nothing

        lax.fori_loop(0, heads, one_head, 0)

    ahead = lax.broadcasted_iota(jnp.int32, (rows, SPAN), 1) - lax.broadcasted_iota(jnp.int32, (rows, SPAN), 0)
    work = []
    for kind, parts in segments:
        valid = [source_of(place) < me for part in parts for place in part[3]]
        if kind == "own":
            work.append((None, parts, [ahead <= 0]))
        elif kind == "row":
            work.append((valid[0], parts, None))
        else:
            work.append((functools.reduce(jnp.logical_or, valid), parts, valid))

    for n, (condition, parts, masks) in enumerate(work):
        if condition is None:
            depth = take_values(parts)
            for head in range(heads):
                begin(head, parts, masks, depth)
            continue
        base_ref = total_ref
        if n == 0:
            base_ref = old_total_ref

            @pl.when(jnp.logical_not(condition))
            def _():
                total_ref[...] = old_total_ref[...]

        pl.when(condition)(functools.partial(quick, parts, masks, base_ref))

    @pl.when(jnp.max(excess_ref[...]) * LOGIT_SCALE > 64.0)
    def _():
        if not first:
            total_ref[...] = old_total_ref[...]
        for condition, parts, masks in work:
            if condition is None:
                depth = take_values(parts)
                for head in range(heads):
                    begin(head, parts, masks, depth)
            else:
                pl.when(condition)(functools.partial(careful, parts, masks))

    if last:
        out_ref = refs[at + 2]
        for head in range(heads):
            total = total_ref[head]
            out_ref[:, head * QDIM : (head + 1) * QDIM] = (
                total[:, :QDIM] / total[:, QDIM:]
            ).astype(jnp.bfloat16)


def attend_step(queries, here, segments, carry, last):
    blocks, described = [], []
    deepest = 0
    for kind, segment in segments:
        parts = []
        for block, offset, size, places in segment:
            at = next((n for n, b in enumerate(blocks) if b is block), None)
            if at is None:
                at = len(blocks)
                blocks.append(block)
            parts.append((at, offset, size, places))
        described.append((kind, parts))
        deepest = max(deepest, sum(part[2] for part in parts))
    first = carry is None
    rows, width = queries.shape
    heads = width // QDIM
    carry_shapes = (
        jax.ShapeDtypeStruct((heads, rows, QDIM), jnp.float32),
        jax.ShapeDtypeStruct((heads, rows, 2 * QDIM), jnp.float32),
    )
    keys = sum(part[2] for _, parts in described for part in parts)
    operands = [here, queries, *blocks]
    aliases = {}
    if not first:
        aliases = {len(operands): 0}
        operands.extend(carry)
    out_shape = carry_shapes
    if last:
        out_shape = carry_shapes + (jax.ShapeDtypeStruct((rows, width), jnp.bfloat16),)
    outputs = pl.pallas_call(
        functools.partial(attend_kernel, described, len(blocks), first, last),
        out_shape=out_shape,
        in_specs=[SMEM] + [VMEM] * (len(operands) - 1),
        out_specs=(VMEM,) * len(out_shape),
        scratch_shapes=[
            pltpu.VMEM((deepest, 2 * QDIM), jnp.bfloat16),
            pltpu.VMEM((rows, QDIM), jnp.float32),
        ],
        input_output_aliases=aliases,
        compiler_params=pltpu.CompilerParams(vmem_limit_bytes=LIMIT),
        cost_estimate=SHORT,
        name="attend",
    )(*operands)
    return outputs[2] if last else outputs


def spread(columns, pair):
    lanes = lax.broadcasted_iota(jnp.int32, (columns.shape[0], 128), 1)
    return jnp.where(lanes < 64, columns[:, 2 * pair : 2 * pair + 1], columns[:, 2 * pair + 1 : 2 * pair + 2])


def triangle(rows):
    down = lax.broadcasted_iota(jnp.int32, (rows, rows), 0)
    along = lax.broadcasted_iota(jnp.int32, (rows, rows), 1)
    return down >= along


def state_kernel(
    x_in, b_in, c_in, decay_in, state_ref, fall_ref, columns_ref, x_ref, b_ref, c_ref, decay_ref, scaled_ref, sems
):
    copies = [
        pltpu.make_async_copy(source, target, sems.at[n])
        for n, (source, target) in enumerate(
            ((decay_in, decay_ref), (x_in, x_ref), (b_in, b_ref), (c_in, c_ref))
        )
    ]
    for copy in copies:
        copy.start()
    for copy in copies:
        copy.wait()
    rows = x_ref.shape[0]
    lower = triangle(rows).astype(jnp.float32)
    columns = lax.dot_general(
        lower, decay_ref[...], (((1,), (1,)), ((), ())), precision=HIGH,
        preferred_element_type=jnp.float32,
    )
    columns_ref[...] = columns
    total = columns[rows - 1 : rows, :]
    remaining = jnp.exp(total - columns)
    fall = jnp.broadcast_to(jnp.exp(total), (8, total.shape[1]))
    for pair in range(x_ref.shape[1] // 128):
        at = slice(pair * 128, (pair + 1) * 128)
        scaled_ref[:, at] = (x_ref[:, at].astype(jnp.float32) * spread(remaining, pair)).astype(jnp.bfloat16)
        fall_ref[:, at] = spread(fall, pair)
    state_ref[...] = lax.dot_general(
        b_ref[...], scaled_ref[...], (((0,), (0,)), ((), ())), preferred_element_type=jnp.float32
    )


def block_states(x, b, c, decay):
    rows, width = x.shape
    heads = decay.shape[0]
    return pl.pallas_call(
        state_kernel,
        out_shape=(
            jax.ShapeDtypeStruct((STATE, width), jnp.float32),
            jax.ShapeDtypeStruct((8, width), jnp.float32),
            jax.ShapeDtypeStruct((rows, heads), jnp.float32),
            jax.ShapeDtypeStruct(x.shape, x.dtype),
            jax.ShapeDtypeStruct(b.shape, b.dtype),
            jax.ShapeDtypeStruct(c.shape, c.dtype),
            jax.ShapeDtypeStruct(decay.shape, decay.dtype),
        ),
        in_specs=[ANY] * 4,
        out_specs=(VMEM,) * 7,
        scratch_shapes=[pltpu.VMEM((rows, width), jnp.bfloat16), pltpu.SemaphoreType.DMA((4,))],
        compiler_params=pltpu.CompilerParams(vmem_limit_bytes=LIMIT),
        cost_estimate=FULL,
        name="states",
    )(x, b, c, decay)


def within_kernel(x_ref, b_ref, c_ref, columns_ref, decay_ref, skip_ref, out_ref):
    rows = x_ref.shape[0]
    causal = triangle(rows)
    scores = lax.dot_general(
        c_ref[...], b_ref[...], (((1,), (1,)), ((), ())), preferred_element_type=jnp.float32
    )
    scores = jnp.where(causal, scores, 0.0)
    upper = jnp.where(causal, 0.0, 1.0) + jnp.where(
        lax.broadcasted_iota(jnp.int32, (rows, rows), 0) == lax.broadcasted_iota(jnp.int32, (rows, rows), 1), 1.0, 0.0
    )
    across = lax.dot_general(
        decay_ref[...], upper, (((1,), (0,)), ((), ())), precision=HIGH,
        preferred_element_type=jnp.float32,
    )
    columns = columns_ref[...]
    lanes = lax.broadcasted_iota(jnp.int32, (rows, 128), 1)
    for pair in range(x_ref.shape[1] // 128):
        at = slice(pair * 128, (pair + 1) * 128)
        x = x_ref[:, at]
        total = None
        for side in range(2):
            head = 2 * pair + side
            gap = jnp.minimum(columns[:, head : head + 1] - across[head : head + 1, :], 0.0)
            weights = (scores * jnp.exp(gap)).astype(jnp.bfloat16)
            mine = lanes < 64 if side == 0 else lanes >= 64
            product = jnp.dot(
                weights, jnp.where(mine, x, jnp.zeros_like(x)), preferred_element_type=jnp.float32
            )
            total = product if total is None else total + product
        out_ref[:, at] = total + skip_ref[:, at] * x.astype(jnp.float32)


def within_blocks(x, b, c, columns, decay, skip):
    rows, width = x.shape
    return pl.pallas_call(
        within_kernel,
        out_shape=jax.ShapeDtypeStruct((rows, width), jnp.float32),
        in_specs=[VMEM] * 6,
        out_specs=VMEM,
        compiler_params=pltpu.CompilerParams(vmem_limit_bytes=LIMIT),
        cost_estimate=FULL,
        name="within",
    )(x, b, c, columns, decay, skip)


def gate_kernel(within_ref, c_ref, carried_ref, columns_ref, gate_ref, gated_ref, squares_ref):
    grown = jnp.exp(columns_ref[...])
    total = None
    for pair in range(within_ref.shape[1] // 128):
        at = slice(pair * 128, (pair + 1) * 128)
        carried = jnp.dot(c_ref[...], carried_ref[:, at], preferred_element_type=jnp.float32)
        values = within_ref[:, at] + carried * spread(grown, pair)
        gate = gate_ref[:, at].astype(jnp.float32)
        gated = values * (gate / (1.0 + jnp.exp(-gate)))
        gated_ref[:, at] = gated
        total = gated * gated if total is None else total + gated * gated
    squares_ref[...] = lax.dot_general(
        jnp.ones((8, 128), jnp.float32), total, (((1,), (1,)), ((), ())), precision=HIGH,
        preferred_element_type=jnp.float32,
    )


def gate_values(within, c, carried, columns, gate):
    rows, width = within.shape
    return pl.pallas_call(
        gate_kernel,
        out_shape=(
            jax.ShapeDtypeStruct((rows, width), jnp.float32),
            jax.ShapeDtypeStruct((8, rows), jnp.float32),
        ),
        in_specs=[VMEM] * 5,
        out_specs=(VMEM, VMEM),
        compiler_params=pltpu.CompilerParams(vmem_limit_bytes=LIMIT),
        cost_estimate=FULL,
        name="gating",
    )(within, c, carried, columns, gate)


def norm_kernel(full_width, gated_ref, squares_ref, gain_ref, out_ref):
    total = lax.dot_general(
        squares_ref[...], jnp.full((8, 128), 0.125, jnp.float32), (((0,), (0,)), ((), ())),
        precision=HIGH, preferred_element_type=jnp.float32,
    )
    factor = lax.rsqrt(total * (1.0 / full_width) + EPSILON)
    for pair in range(gated_ref.shape[1] // 128):
        at = slice(pair * 128, (pair + 1) * 128)
        out_ref[:, at] = (gated_ref[:, at] * factor * gain_ref[:, at]).astype(jnp.bfloat16)


def normalize(gated, squares, gain, full_width):
    rows, width = gated.shape
    return pl.pallas_call(
        functools.partial(norm_kernel, full_width),
        out_shape=jax.ShapeDtypeStruct((rows, width), jnp.bfloat16),
        in_specs=[VMEM] * 3,
        out_specs=VMEM,
        compiler_params=pltpu.CompilerParams(vmem_limit_bytes=LIMIT),
        cost_estimate=FULL,
        name="normalize",
    )(gated, squares, gain)


def packed(state, fall):
    high = lax.reduce_precision(fall, 8, 7)
    return jnp.concatenate([state, high, fall - high], axis=0).astype(jnp.bfloat16)


def unpacked(message):
    wide = message.astype(jnp.float32)
    return wide[:STATE], wide[STATE : STATE + 8] + wide[STATE + 8 : STATE + 16]


def once(value, *others):
    return lax.optimization_barrier((value, *others))[0]


def entering_state(state, fall, me, needs, turns):
    kept = []
    needs, turns = iter(needs), iter(turns)
    for level in range(3):
        upper = (me >> level) & 1 == 1
        width = state.shape[1] // 2
        low, high = state[:, :width], state[:, width:]
        fall_low, fall_high = fall[:, :width], fall[:, width:]
        mine, mine_fall = jnp.where(upper, high, low), jnp.where(upper, fall_high, fall_low)
        message = packed(jnp.where(upper, low, high), jnp.where(upper, fall_low, fall_high))
        received = across_z(once(message, *next(needs)), 1 << level)
        turn = next(turns)
        if callable(turn):
            turn = turn(received)
        theirs, their_fall = unpacked(once(received, *turn))
        before, after = jnp.where(upper, theirs, mine), jnp.where(upper, mine, theirs)
        before_fall = jnp.where(upper, their_fall, mine_fall)
        after_fall = jnp.where(upper, mine_fall, their_fall)
        kept.append((upper, before, before_fall))
        state = after_fall[:1] * before + after
        fall = before_fall * after_fall
    message = once(packed(state, fall), *next(needs))
    moved = [along_y(message, 1), along_y(message, -1), along_y(message, 2)]
    moved = lax.optimization_barrier((*moved, *next(turns)))[:3]
    (one, one_fall), (three, _), (two, two_fall) = (unpacked(block) for block in moved)
    y_at = lax.shift_right_logical(me, 3)
    one, two, three = (jnp.where(y_at >= n, block, 0.0) for n, block in ((1, one), (2, two), (3, three)))
    entering = one + one_fall[:1] * (two + two_fall[:1] * three)
    for level in reversed(range(3)):
        upper, before, before_fall = kept[level]
        second = before_fall[:1] * entering + before
        mine = jnp.where(upper, second, entering)
        other = jnp.where(upper, entering, second).astype(jnp.bfloat16)
        received = once(across_z(once(other, *next(needs)), 1 << level), *next(turns)).astype(jnp.float32)
        entering = jnp.where(
            upper,
            jnp.concatenate([received, mine], axis=1),
            jnp.concatenate([mine, received], axis=1),
        )
    return entering.astype(jnp.bfloat16)


def sum_over_heads(squares, turns):
    devices = lax.axis_size("head")

    def moved(block, bits):
        return lax.ppermute(block, "head", [(i, i ^ bits) for i in range(devices)])

    squares = squares + once(moved(squares, 1), *turns[0])
    others = [moved(squares, 2 * n) for n in range(1, devices // 2)]
    return sum(lax.optimization_barrier((*others, *turns[1]))[: len(others)], squares)


def body(
    mixer_input, gate_input, input_b, input_c, log_decay, skip_gain, norm_gain, queries, key_rows, value_rows
):
    me = lax.axis_index("seq").astype(jnp.int32)
    here = me[None]
    head_width = mixer_input.shape[1] // skip_gain.shape[0]
    full_width = mixer_input.shape[1] * lax.axis_size("head")

    own = prepare(key_rows, value_rows)
    state, fall, columns, x, b, c, decay = block_states(mixer_input, input_b, input_c, log_decay)

    up, down = [own], [own]
    for step in range(4):
        up.append(along_z(up[-1], 1))
        if step < 3:
            down.append(along_z(down[-1], -1))
    parts = [[(0, own), (-1, up[1]), (1, down[1])], [(-2, up[2]), (2, down[2]), (-3, up[3]), (3, down[3]), (-4, up[4])]]
    packs = [jnp.concatenate([block for _, block in part], axis=0) for part in parts]
    above = [along_y(pack, 1) for pack in packs]
    below = [along_y(pack, -1) for pack in packs]
    across = [along_y(above[0], 1), along_y(below[1], -1)]

    def from_row(which, blocks, row, start=0, stop=None):
        places = [(row, z) for z, _ in parts[which]][start:stop]
        return ("row", [(blocks[which], start * SPAN, len(places) * SPAN, places)])

    withins = []

    def compute_within(received):
        spread_skip = jnp.repeat(skip_gain, head_width)[None, :]
        withins.append(within_blocks(once(x, received), b, c, columns, decay, spread_skip))
        needs[1].append(withins[0])
        return []

    def near(part):
        return ("blocks", [(block, 0, SPAN, [(0, z)]) for z, block in part])

    steps = [
        [("own", [(own, 0, SPAN, [(0, 0)])]), near(parts[0][1:] + parts[1][:2])],
        [near(parts[1][2:4]), from_row(0, above, -1)],
        [near(parts[1][4:]), from_row(0, below, 1)],
        [from_row(1, above, -1)],
        [from_row(1, below, 1)],
        [from_row(0, across, 2)],
        [from_row(1, across, 2, 0, 3)],
        [from_row(1, across, 2, 3, 5)],
    ]
    carry, done = None, []
    for at, segments in enumerate(steps):
        carry = attend_step(queries, here, segments, carry, at == len(steps) - 1)
        done.append(carry if at == len(steps) - 1 else carry[0])
    needs = [[], [up[2], down[2]], [up[3], down[3]], [up[4]], [], [], []]
    turns = [compute_within] + [[done[n]] for n in range(6)]
    carried = entering_state(state, fall, me, needs, turns)
    attended = done[-1]

    gated, squares = gate_values(withins[0], c, carried, columns, gate_input)
    squares = sum_over_heads(squares, [[done[6]], [done[7]]])
    mixer_output = normalize(gated, squares, norm_gain[None, :], full_width)
    return (mixer_output, attended)


def solution(mesh):
    return jax.shard_map(
        body,
        mesh=mesh,
        in_specs=(
            P("seq", "head"),
            P("seq", "head"),
            P("seq", "head"),
            P("seq", "head"),
            P("head", "seq"),
            P("head"),
            P("head"),
            P("seq", "head"),
            P("seq", "head"),
            P("seq", "head"),
        ),
        out_specs=(P("seq", "head"), P("seq", "head")),
        check_vma=False,
    )
```

```python
import functools
import math

import jax
import jax.numpy as jnp
from jax import lax
from jax.experimental import pallas as pl
from jax.experimental.pallas import tpu as pltpu
from jax.sharding import PartitionSpec as P

STATE = 128
QDIM = 128
SPAN = 256
EPSILON = 1e-05
SEQ_Y, SEQ_Z = 4, 8
LOGIT_SCALE = QDIM ** (-0.5) * math.log2(math.e)
HIGH = lax.Precision.HIGHEST
VMEM = pl.BlockSpec(memory_space=pltpu.VMEM)
ANY = pl.BlockSpec(memory_space=pl.ANY)
SMEM = pl.BlockSpec(memory_space=pltpu.SMEM)
LIMIT = 40 * 2**20


def send(block, target):
    route = []
    for y in range(SEQ_Y):
        for z in range(SEQ_Z):
            to = target(y, z)
            if to is not None:
                route.append((y * SEQ_Z + z, to[0] * SEQ_Z + to[1]))
    return lax.ppermute(block, "seq", route)


def along_z(block, distance):
    return send(block, lambda y, z: (y, (z + distance) % SEQ_Z))


def along_y(block, distance):
    return send(block, lambda y, z: ((y + distance) % SEQ_Y, z))


def later_y(block, distance):
    return send(block, lambda y, z: (y + distance, z) if y + distance < SEQ_Y else None)


def across_z(block, bit):
    return send(block, lambda y, z: (y, z ^ bit))


SHORT = pl.CostEstimate(flops=5 * 10**8, bytes_accessed=2**16, transcendentals=0)
FULL = pl.CostEstimate(flops=2 * 10**9, bytes_accessed=2**16, transcendentals=0)


def prepare_kernel(key_ref, value_ref, out_ref, sems):
    copies = [
        pltpu.make_async_copy(source, out_ref.at[:, n * QDIM : (n + 1) * QDIM], sems.at[n])
        for n, source in enumerate((key_ref, value_ref))
    ]
    for copy in copies:
        copy.start()
    for copy in copies:
        copy.wait()


def prepare(key_rows, value_rows):
    return pl.pallas_call(
        prepare_kernel,
        out_shape=jax.ShapeDtypeStruct((SPAN, 2 * QDIM), jnp.bfloat16),
        in_specs=[ANY, ANY],
        out_specs=VMEM,
        scratch_shapes=[pltpu.SemaphoreType.DMA((2,))],
        cost_estimate=FULL,
        name="prepare",
    )(key_rows, value_rows)


def attend_kernel(segments, count, first, last, *refs):
    here_ref, query_ref = refs[0], refs[1]
    blocks = refs[2 : 2 + count]
    at = 2 + count
    old_total_ref = None
    if not first:
        old_total_ref = refs[at + 1]
        at += 2
    max_ref, total_ref = refs[at : at + 2]
    wide_ref, excess_ref = refs[-2:]
    heads = query_ref.shape[1] // QDIM
    rows = query_ref.shape[0]
    me = here_ref[0]
    my_y, my_z = lax.shift_right_logical(me, 3), lax.bitwise_and(me, SEQ_Z - 1)

    def source_of(place):
        up, along = place
        source_y = lax.bitwise_and(my_y + (up + SEQ_Y), SEQ_Y - 1)
        return source_y * SEQ_Z + lax.bitwise_and(my_z + (along + SEQ_Z), SEQ_Z - 1)

    wide_ref[:, QDIM:] = jnp.ones((wide_ref.shape[0], QDIM), jnp.bfloat16)
    excess_ref[...] = jnp.zeros(excess_ref.shape, jnp.float32)

    def take_values(parts):
        place = 0
        for which, offset, size, _ in parts:
            wide_ref[place : place + size, :QDIM] = blocks[which][offset : offset + size, QDIM:]
            place += size
        return place

    def first_product(head, parts, masks):
        if isinstance(head, int):
            query = query_ref[:, head * QDIM : (head + 1) * QDIM]
        else:
            query = query_ref[:, pl.ds(pl.multiple_of(head * QDIM, QDIM), QDIM)]
        pieces = []
        for which, offset, size, _ in parts:
            keys = blocks[which][offset : offset + size, :QDIM]
            pieces.append(
                lax.dot_general(query, keys, (((1,), (1,)), ((), ())), preferred_element_type=jnp.float32)
            )
        if masks is not None:
            pieces = [
                jnp.where(masks[at], piece, -1e30)
                for at, piece in enumerate(
                    piece[:, n * SPAN : (n + 1) * SPAN]
                    for piece in pieces
                    for n in range(piece.shape[1] // SPAN)
                )
            ]
        return pieces[0] if len(pieces) == 1 else jnp.concatenate(pieces, axis=1)

    def weigh(logits, largest):
        return jnp.exp2(logits * LOGIT_SCALE - (largest * LOGIT_SCALE)[:, :1]).astype(jnp.bfloat16)

    def begin(head, parts, masks, depth):
        logits = first_product(head, parts, masks)
        largest = jnp.broadcast_to(jnp.max(logits, axis=1, keepdims=True), (rows, QDIM))
        max_ref[head] = largest
        total_ref[head] = jnp.dot(
            weigh(logits, largest), wide_ref[:depth, :], preferred_element_type=jnp.float32
        )

    def quick(parts, masks, base_ref):
        depth = take_values(parts)
        excess = None
        following = first_product(0, parts, masks)
        for head in range(heads):
            logits = following
            if head + 1 < heads:
                following = first_product(head + 1, parts, masks)
            largest = max_ref[head]
            total_ref[head] = base_ref[head] + jnp.dot(
                weigh(logits, largest), wide_ref[:depth, :], preferred_element_type=jnp.float32
            )
            columns = [logits[:, n * QDIM : (n + 1) * QDIM] for n in range(depth // QDIM)]
            over = functools.reduce(jnp.maximum, columns) - largest
            excess = over if excess is None else jnp.maximum(excess, over)
        excess_ref[...] = jnp.maximum(excess_ref[...], excess)

    def careful(parts, masks):
        depth = take_values(parts)

        def one_head(head, nothing):
            logits = first_product(head, parts, masks)
            old = max_ref[head]
            new = jnp.maximum(old, jnp.max(logits, axis=1, keepdims=True))
            max_ref[head] = new
            rescale = jnp.exp2(old * LOGIT_SCALE - new * LOGIT_SCALE)
            total_ref[head] = total_ref[head] * rescale[:, :1] + jnp.dot(
                weigh(logits, new), wide_ref[:depth, :], preferred_element_type=jnp.float32
            )
            return nothing

        lax.fori_loop(0, heads, one_head, 0)

    ahead = lax.broadcasted_iota(jnp.int32, (rows, SPAN), 1) - lax.broadcasted_iota(jnp.int32, (rows, SPAN), 0)
    work = []
    for kind, parts in segments:
        valid = [source_of(place) < me for part in parts for place in part[3]]
        if kind == "own":
            work.append((None, parts, [ahead <= 0]))
        elif kind == "row":
            work.append((valid[0], parts, None))
        else:
            work.append((functools.reduce(jnp.logical_or, valid), parts, valid))

    for n, (condition, parts, masks) in enumerate(work):
        if condition is None:
            depth = take_values(parts)
            for head in range(heads):
                begin(head, parts, masks, depth)
            continue
        base_ref = total_ref
        if n == 0:
            base_ref = old_total_ref

            @pl.when(jnp.logical_not(condition))
            def _():
                total_ref[...] = old_total_ref[...]

        pl.when(condition)(functools.partial(quick, parts, masks, base_ref))

    @pl.when(jnp.max(excess_ref[...]) * LOGIT_SCALE > 64.0)
    def _():
        if not first:
            total_ref[...] = old_total_ref[...]
        for condition, parts, masks in work:
            if condition is None:
                depth = take_values(parts)
                for head in range(heads):
                    begin(head, parts, masks, depth)
            else:
                pl.when(condition)(functools.partial(careful, parts, masks))

    if last:
        out_ref = refs[at + 2]
        for head in range(heads):
            total = total_ref[head]
            out_ref[:, head * QDIM : (head + 1) * QDIM] = (
                total[:, :QDIM] / total[:, QDIM:]
            ).astype(jnp.bfloat16)


def attend_step(queries, here, segments, carry, last):
    blocks, described = [], []
    deepest = 0
    for kind, segment in segments:
        parts = []
        for block, offset, size, places in segment:
            at = next((n for n, b in enumerate(blocks) if b is block), None)
            if at is None:
                at = len(blocks)
                blocks.append(block)
            parts.append((at, offset, size, places))
        described.append((kind, parts))
        deepest = max(deepest, sum(part[2] for part in parts))
    first = carry is None
    rows, width = queries.shape
    heads = width // QDIM
    carry_shapes = (
        jax.ShapeDtypeStruct((heads, rows, QDIM), jnp.float32),
        jax.ShapeDtypeStruct((heads, rows, 2 * QDIM), jnp.float32),
    )
    keys = sum(part[2] for _, parts in described for part in parts)
    operands = [here, queries, *blocks]
    aliases = {}
    if not first:
        aliases = {len(operands): 0}
        operands.extend(carry)
    out_shape = carry_shapes
    if last:
        out_shape = carry_shapes + (jax.ShapeDtypeStruct((rows, width), jnp.bfloat16),)
    outputs = pl.pallas_call(
        functools.partial(attend_kernel, described, len(blocks), first, last),
        out_shape=out_shape,
        in_specs=[SMEM] + [VMEM] * (len(operands) - 1),
        out_specs=(VMEM,) * len(out_shape),
        scratch_shapes=[
            pltpu.VMEM((deepest, 2 * QDIM), jnp.bfloat16),
            pltpu.VMEM((rows, QDIM), jnp.float32),
        ],
        input_output_aliases=aliases,
        compiler_params=pltpu.CompilerParams(vmem_limit_bytes=LIMIT),
        cost_estimate=SHORT,
        name="attend",
    )(*operands)
    return outputs[2] if last else outputs


def spread(columns, pair):
    lanes = lax.broadcasted_iota(jnp.int32, (columns.shape[0], 128), 1)
    return jnp.where(lanes < 64, columns[:, 2 * pair : 2 * pair + 1], columns[:, 2 * pair + 1 : 2 * pair + 2])


def triangle(rows):
    down = lax.broadcasted_iota(jnp.int32, (rows, rows), 0)
    along = lax.broadcasted_iota(jnp.int32, (rows, rows), 1)
    return down >= along


def state_kernel(
    x_in, b_in, c_in, decay_in, state_ref, fall_ref, columns_ref, x_ref, b_ref, c_ref, decay_ref, scaled_ref, sems
):
    copies = [
        pltpu.make_async_copy(source, target, sems.at[n])
        for n, (source, target) in enumerate(
            ((decay_in, decay_ref), (x_in, x_ref), (b_in, b_ref), (c_in, c_ref))
        )
    ]
    for copy in copies:
        copy.start()
    for copy in copies:
        copy.wait()
    rows = x_ref.shape[0]
    lower = triangle(rows).astype(jnp.float32)
    columns = lax.dot_general(
        lower, decay_ref[...], (((1,), (1,)), ((), ())), precision=HIGH,
        preferred_element_type=jnp.float32,
    )
    columns_ref[...] = columns
    total = columns[rows - 1 : rows, :]
    remaining = jnp.exp(total - columns)
    fall = jnp.broadcast_to(jnp.exp(total), (8, total.shape[1]))
    for pair in range(x_ref.shape[1] // 128):
        at = slice(pair * 128, (pair + 1) * 128)
        scaled_ref[:, at] = (x_ref[:, at].astype(jnp.float32) * spread(remaining, pair)).astype(jnp.bfloat16)
        fall_ref[:, at] = spread(fall, pair)
    state_ref[...] = lax.dot_general(
        b_ref[...], scaled_ref[...], (((0,), (0,)), ((), ())), preferred_element_type=jnp.float32
    )


def block_states(x, b, c, decay):
    rows, width = x.shape
    heads = decay.shape[0]
    return pl.pallas_call(
        state_kernel,
        out_shape=(
            jax.ShapeDtypeStruct((STATE, width), jnp.float32),
            jax.ShapeDtypeStruct((8, width), jnp.float32),
            jax.ShapeDtypeStruct((rows, heads), jnp.float32),
            jax.ShapeDtypeStruct(x.shape, x.dtype),
            jax.ShapeDtypeStruct(b.shape, b.dtype),
            jax.ShapeDtypeStruct(c.shape, c.dtype),
            jax.ShapeDtypeStruct(decay.shape, decay.dtype),
        ),
        in_specs=[ANY] * 4,
        out_specs=(VMEM,) * 7,
        scratch_shapes=[pltpu.VMEM((rows, width), jnp.bfloat16), pltpu.SemaphoreType.DMA((4,))],
        compiler_params=pltpu.CompilerParams(vmem_limit_bytes=LIMIT),
        cost_estimate=FULL,
        name="states",
    )(x, b, c, decay)


def within_kernel(x_ref, b_ref, c_ref, columns_ref, decay_ref, skip_ref, out_ref):
    rows = x_ref.shape[0]
    causal = triangle(rows)
    scores = lax.dot_general(
        c_ref[...], b_ref[...], (((1,), (1,)), ((), ())), preferred_element_type=jnp.float32
    )
    scores = jnp.where(causal, scores, 0.0)
    upper = jnp.where(causal, 0.0, 1.0) + jnp.where(
        lax.broadcasted_iota(jnp.int32, (rows, rows), 0) == lax.broadcasted_iota(jnp.int32, (rows, rows), 1), 1.0, 0.0
    )
    across = lax.dot_general(
        decay_ref[...], upper, (((1,), (0,)), ((), ())), precision=HIGH,
        preferred_element_type=jnp.float32,
    )
    columns = columns_ref[...]
    lanes = lax.broadcasted_iota(jnp.int32, (rows, 128), 1)
    for pair in range(x_ref.shape[1] // 128):
        at = slice(pair * 128, (pair + 1) * 128)
        x = x_ref[:, at]
        total = None
        for side in range(2):
            head = 2 * pair + side
            gap = jnp.minimum(columns[:, head : head + 1] - across[head : head + 1, :], 0.0)
            weights = (scores * jnp.exp(gap)).astype(jnp.bfloat16)
            mine = lanes < 64 if side == 0 else lanes >= 64
            product = jnp.dot(
                weights, jnp.where(mine, x, jnp.zeros_like(x)), preferred_element_type=jnp.float32
            )
            total = product if total is None else total + product
        out_ref[:, at] = total + skip_ref[:, at] * x.astype(jnp.float32)


def within_blocks(x, b, c, columns, decay, skip):
    rows, width = x.shape
    return pl.pallas_call(
        within_kernel,
        out_shape=jax.ShapeDtypeStruct((rows, width), jnp.float32),
        in_specs=[VMEM] * 6,
        out_specs=VMEM,
        compiler_params=pltpu.CompilerParams(vmem_limit_bytes=LIMIT),
        cost_estimate=FULL,
        name="within",
    )(x, b, c, columns, decay, skip)


def gate_kernel(within_ref, c_ref, carried_ref, columns_ref, gate_ref, gated_ref, squares_ref):
    grown = jnp.exp(columns_ref[...])
    total = None
    for pair in range(within_ref.shape[1] // 128):
        at = slice(pair * 128, (pair + 1) * 128)
        carried = jnp.dot(c_ref[...], carried_ref[:, at], preferred_element_type=jnp.float32)
        values = within_ref[:, at] + carried * spread(grown, pair)
        gate = gate_ref[:, at].astype(jnp.float32)
        gated = values * (gate / (1.0 + jnp.exp(-gate)))
        gated_ref[:, at] = gated
        total = gated * gated if total is None else total + gated * gated
    squares_ref[...] = lax.dot_general(
        jnp.ones((8, 128), jnp.float32), total, (((1,), (1,)), ((), ())), precision=HIGH,
        preferred_element_type=jnp.float32,
    )


def gate_values(within, c, carried, columns, gate):
    rows, width = within.shape
    return pl.pallas_call(
        gate_kernel,
        out_shape=(
            jax.ShapeDtypeStruct((rows, width), jnp.float32),
            jax.ShapeDtypeStruct((8, rows), jnp.float32),
        ),
        in_specs=[VMEM] * 5,
        out_specs=(VMEM, VMEM),
        compiler_params=pltpu.CompilerParams(vmem_limit_bytes=LIMIT),
        cost_estimate=FULL,
        name="gating",
    )(within, c, carried, columns, gate)


def norm_kernel(full_width, gated_ref, squares_ref, gain_ref, out_ref):
    total = lax.dot_general(
        squares_ref[...], jnp.full((8, 128), 0.125, jnp.float32), (((0,), (0,)), ((), ())),
        precision=HIGH, preferred_element_type=jnp.float32,
    )
    factor = lax.rsqrt(total * (1.0 / full_width) + EPSILON)
    for pair in range(gated_ref.shape[1] // 128):
        at = slice(pair * 128, (pair + 1) * 128)
        out_ref[:, at] = (gated_ref[:, at] * factor * gain_ref[:, at]).astype(jnp.bfloat16)


def normalize(gated, squares, gain, full_width):
    rows, width = gated.shape
    return pl.pallas_call(
        functools.partial(norm_kernel, full_width),
        out_shape=jax.ShapeDtypeStruct((rows, width), jnp.bfloat16),
        in_specs=[VMEM] * 3,
        out_specs=VMEM,
        compiler_params=pltpu.CompilerParams(vmem_limit_bytes=LIMIT),
        cost_estimate=FULL,
        name="normalize",
    )(gated, squares, gain)


def packed(state, fall):
    high = lax.reduce_precision(fall, 8, 7)
    return jnp.concatenate([state, high, fall - high], axis=0).astype(jnp.bfloat16)


def unpacked(message):
    wide = message.astype(jnp.float32)
    return wide[:STATE], wide[STATE : STATE + 8] + wide[STATE + 8 : STATE + 16]


def once(value, *others):
    return lax.optimization_barrier((value, *others))[0]


def entering_state(state, fall, me, needs, turns):
    kept = []
    needs, turns = iter(needs), iter(turns)
    for level in range(3):
        upper = (me >> level) & 1 == 1
        width = state.shape[1] // 2
        low, high = state[:, :width], state[:, width:]
        fall_low, fall_high = fall[:, :width], fall[:, width:]
        mine, mine_fall = jnp.where(upper, high, low), jnp.where(upper, fall_high, fall_low)
        message = packed(jnp.where(upper, low, high), jnp.where(upper, fall_low, fall_high))
        received = across_z(once(message, *next(needs)), 1 << level)
        turn = next(turns)
        if callable(turn):
            turn = turn(received)
        theirs, their_fall = unpacked(once(received, *turn))
        before, after = jnp.where(upper, theirs, mine), jnp.where(upper, mine, theirs)
        before_fall = jnp.where(upper, their_fall, mine_fall)
        after_fall = jnp.where(upper, mine_fall, their_fall)
        kept.append((upper, before, before_fall))
        state = after_fall[:1] * before + after
        fall = before_fall * after_fall
    message = once(packed(state, fall), *next(needs))
    moved = [along_y(message, 1), along_y(message, -1), along_y(message, 2)]
    moved = lax.optimization_barrier((*moved, *next(turns)))[:3]
    (one, one_fall), (three, _), (two, two_fall) = (unpacked(block) for block in moved)
    y_at = lax.shift_right_logical(me, 3)
    one, two, three = (jnp.where(y_at >= n, block, 0.0) for n, block in ((1, one), (2, two), (3, three)))
    entering = one + one_fall[:1] * (two + two_fall[:1] * three)
    for level in reversed(range(3)):
        upper, before, before_fall = kept[level]
        second = before_fall[:1] * entering + before
        mine = jnp.where(upper, second, entering)
        other = jnp.where(upper, entering, second).astype(jnp.bfloat16)
        received = once(across_z(once(other, *next(needs)), 1 << level), *next(turns)).astype(jnp.float32)
        entering = jnp.where(
            upper,
            jnp.concatenate([received, mine], axis=1),
            jnp.concatenate([mine, received], axis=1),
        )
    return entering.astype(jnp.bfloat16)


def sum_over_heads(squares, turns):
    devices = lax.axis_size("head")

    def moved(block, bits):
        return lax.ppermute(block, "head", [(i, i ^ bits) for i in range(devices)])

    squares = squares + once(moved(squares, 1), *turns[0])
    others = [moved(squares, 2 * n) for n in range(1, devices // 2)]
    return sum(lax.optimization_barrier((*others, *turns[1]))[: len(others)], squares)


def body(
    mixer_input, gate_input, input_b, input_c, log_decay, skip_gain, norm_gain, queries, key_rows, value_rows
):
    me = lax.axis_index("seq").astype(jnp.int32)
    here = me[None]
    head_width = mixer_input.shape[1] // skip_gain.shape[0]
    full_width = mixer_input.shape[1] * lax.axis_size("head")

    own = prepare(key_rows, value_rows)
    state, fall, columns, x, b, c, decay = block_states(mixer_input, input_b, input_c, log_decay)

    up, down = [own], [own]
    for step in range(4):
        up.append(along_z(up[-1], 1))
        if step < 3:
            down.append(along_z(down[-1], -1))
    parts = [[(0, own), (-1, up[1]), (1, down[1])], [(-2, up[2]), (2, down[2]), (-3, up[3]), (3, down[3]), (-4, up[4])]]
    packs = [once(jnp.concatenate([block for _, block in parts[0]], axis=0), up[2], down[2]), None]
    above, below = [along_y(packs[0], 1)], [along_y(packs[0], -1)]
    across = [along_y(above[0], 1)]

    def from_row(which, blocks, row, start=0, stop=None):
        places = [(row, z) for z, _ in parts[which]][start:stop]
        return ("row", [(blocks[which], start * SPAN, len(places) * SPAN, places)])

    withins = []

    def compute_within(received):
        spread_skip = jnp.repeat(skip_gain, head_width)[None, :]
        withins.append(within_blocks(once(x, received), b, c, columns, decay, spread_skip))
        needs[1].append(withins[0])
        return []

    def near(part):
        return ("blocks", [(block, 0, SPAN, [(0, z)]) for z, block in part])

    carries, done = [None], []

    def step(segments, last=False):
        carries.append(attend_step(queries, here, segments, carries[-1], last))
        done.append(carries[-1] if last else carries[-1][0])

    step([("own", [(own, 0, SPAN, [(0, 0)])]), near(parts[0][1:] + parts[1][:2])])
    step([near(parts[1][2:4]), from_row(0, above, -1)])
    parts[1][4] = (-4, once(up[4], done[1]))
    packs[1] = jnp.concatenate([block for _, block in parts[1]], axis=0)
    above.append(along_y(packs[1], 1))
    below.append(along_y(packs[1], -1))
    across.append(along_y(below[1], -1))
    step([near(parts[1][4:]), from_row(0, below, 1)])
    step([from_row(1, above, -1)])
    step([from_row(1, below, 1)])
    step([from_row(0, across, 2)])
    step([from_row(1, across, 2, 0, 3)])
    step([from_row(1, across, 2, 3, 5)], True)
    needs = [[], [up[2], down[2]], [up[3], down[3]], [parts[1][4][1]], [], [], []]
    turns = [compute_within] + [[done[n]] for n in range(6)]
    carried = entering_state(state, fall, me, needs, turns)
    attended = done[-1]

    gated, squares = gate_values(withins[0], c, carried, columns, gate_input)
    squares = sum_over_heads(squares, [[done[6]], [done[7]]])
    mixer_output = normalize(gated, squares, norm_gain[None, :], full_width)
    return (mixer_output, attended)


def solution(mesh):
    return jax.shard_map(
        body,
        mesh=mesh,
        in_specs=(
            P("seq", "head"),
            P("seq", "head"),
            P("seq", "head"),
            P("seq", "head"),
            P("head", "seq"),
            P("head"),
            P("head"),
            P("seq", "head"),
            P("seq", "head"),
            P("seq", "head"),
        ),
        out_specs=(P("seq", "head"), P("seq", "head")),
        check_vma=False,
    )
```
